256 devices in a mesh: head: 4 (over x), ctx: 64 (over y, z, core).
Axes of the slice: x: 4, y: 4, z: 8, core: 2. Of those that a mesh axis runs over, the one named last changes fastest.
Arguments:
- queries: bfloat16 [256, 8192], P(('head', 'ctx')), may hold values from -2.5 to 2.5
- d_out: bfloat16 [256, 8192], P(('head', 'ctx')), may hold values from -384 to 384
- out_rows: bfloat16 [256, 8192], P(('head', 'ctx')), may hold values from -6 to 6
- lse: bfloat16 [256, 64], P(('head', 'ctx')), may hold values from 9 to 12
- lengths: int32 [4], replicated, may hold values from 1 to 64, 160 in all
- keys: bfloat16 [131072, 1024], P('ctx', 'head'), may hold values from -2.5 to 2.5
- values: bfloat16 [131072, 1024], P('ctx', 'head'), may hold values from -6 to 6
Outputs:
- d_queries: bfloat16 [256, 8192], P(('head', 'ctx'))
- d_keys: bfloat16 [131072, 1024], P('ctx', 'head')
- d_values: bfloat16 [131072, 1024], P('ctx', 'head')
The draws below stay inside these ranges and needn't reach their ends.
Inputs may be any that keep to these rules, and one draw needn't show every extreme that they name: lengths of samples; they sum to exactly 160 and the largest is exactly 64.
All inputs are finite; a program needn't handle non-finite values.
Results may differ from the reference program's by a relative error of at most 0.0085.
Values may be sent and summed in bfloat16 or wider, within the bound.
A program may use at most 128 MiB of HBM per device.

```python
import math
import jax
import jax.numpy as jnp
import numpy as np
from jax import lax

HQ = 64
KVH = 8
DH = 128
SPAN = 64
SAMPLES = 4
CTX_DEV = 2048
ROWS = 256
LIVE = 160
PROMPT = 131072
N_CTX = 64


def level_of(rng, shape, shards, low, top_value):
    def one(axis_at, shards_of):
        steps = jax.random.uniform(jax.random.fold_in(jax.random.fold_in(rng, 6), axis_at), (shards_of,), jnp.float32, low / len(shards), top_value / len(shards))
        return jnp.repeat(jnp.exp(steps), shape[axis_at] // shards_of).reshape((-1,) + (1,) * (len(shape) - axis_at - 1))

    level = one(*shards[0])
    for cut in shards[1:]:
        level = level * one(*cut)
    return level


def length_profile(count, total, reach, skew):
    weights = [(1 << 20) // math.isqrt(grade ** skew) + 1 for grade in range(2, count + 1)]
    surplus, given = total - reach - (count - 1), [1] * (count - 1)
    while surplus > 0:
        candidates = [i for i in range(count - 1) if given[i] < reach]
        pool, remaining = sum([weights[i] for i in candidates]), surplus
        for i in candidates:
            addition = min(reach - given[i], max(1, remaining * weights[i] // pool), surplus)
            given[i] = given[i] + addition
            surplus = surplus - addition
    return np.array([reach] + given)


def uneven_parts(key, amount, total, most, slope):
    if amount == 2:
        one = jax.random.randint(key, (), max(1, total - most), min(most, total - 1) + 1)
        return jnp.stack([one, total - one])
    tallies = jnp.asarray(length_profile(amount, total, most, slope), jnp.int32)
    twos = (amount - 1) // 2
    source_of, sink = tallies[1:1 + 2 * twos:2], tallies[2:2 + 2 * twos:2]
    margin = jnp.minimum(source_of - 1, most - sink)
    passed = jax.random.randint(jax.random.fold_in(key, 1), (twos,), 0, 1 << 20) % (margin + 1)
    tallies = tallies.at[1:1 + 2 * twos:2].set(source_of - passed).at[2:2 + 2 * twos:2].set(sink + passed)
    return tallies[jax.random.permutation(jax.random.fold_in(key, 2), amount)]


def centred(key, extent, spread, limit, split=(), held_as=jnp.bfloat16):
    values = jax.random.normal(key, extent, jnp.float32) * spread
    if len(split) > 0:
        values = level_of(key, extent, split, -0.22, 0.18) * values
    return jnp.clip(values, min=-limit, max=limit).astype(held_as)


def setup_inputs(seed: int = 0) -> dict:
    arg_keys = jax.random.split(jax.random.key(seed), 8)
    queries = centred(arg_keys[0], (ROWS, HQ * DH), 1.0, 2.5, ((0, 256),))
    d_out = centred(arg_keys[1], (ROWS, HQ * DH), 64.0, 384.0, ((0, 256),))
    out_rows = centred(arg_keys[2], (ROWS, HQ * DH), 1.0, 6.0, ((0, 256),))
    lse = jnp.clip(9.0 + 3.0 * jax.random.uniform(arg_keys[3], (ROWS, HQ), jnp.float32) ** level_of(arg_keys[3], (ROWS, HQ), ((0, 256),), -0.2, 0.2), 9.0, 12.0).astype(jnp.bfloat16)
    lengths = uneven_parts(arg_keys[4], SAMPLES, LIVE, SPAN, 2).astype(jnp.int32)
    keys = centred(arg_keys[5], (PROMPT, KVH * DH), 1.0, 2.5, ((0, 64), (1, 4)))
    values = centred(arg_keys[6], (PROMPT, KVH * DH), 1.0, 6.0, ((0, 64), (1, 4)))
    return {"queries": queries, "d_out": d_out, "out_rows": out_rows, "lse": lse, "lengths": lengths, "keys": keys, "values": values}


def reference(queries, d_out, out_rows, lse, lengths, keys, values):
    scale = 1.0 / (DH ** 0.5)
    group = HQ // KVH
    position = jnp.arange(ROWS, dtype=jnp.int32)
    sample = position // SPAN
    live = (position % SPAN) < lengths[sample]
    masked = jnp.where(live[:, None], d_out, jnp.zeros_like(d_out))
    q_heads = queries.astype(jnp.float32).reshape(ROWS, KVH, group, DH)
    m_heads = masked.astype(jnp.float32).reshape(ROWS, KVH, group, DH)
    o_heads = out_rows.astype(jnp.float32).reshape(ROWS, KVH, group, DH)
    delta = jnp.sum(m_heads * o_heads, axis=-1)
    lse_heads = lse.astype(jnp.float32).reshape(ROWS, KVH, group)
    key_tiles = keys.reshape(N_CTX, CTX_DEV, KVH, DH)
    value_tiles = values.reshape(N_CTX, CTX_DEV, KVH, DH)

    def step(d_query, tiles):
        key_tile = tiles[0].astype(jnp.float32)
        value_tile = tiles[1].astype(jnp.float32)
        scores = jnp.einsum('rgjd,pgd->rgjp', q_heads, key_tile) * scale
        weights = jnp.exp(scores - lse_heads[..., None])
        probs = lax.optimization_barrier(weights.astype(jnp.bfloat16)).astype(jnp.float32)
        d_weights = jnp.einsum('rgjd,pgd->rgjp', m_heads, value_tile)
        d_scores = lax.optimization_barrier((weights * (d_weights - delta[..., None])).astype(jnp.bfloat16)).astype(jnp.float32)
        d_value = jnp.einsum('rgjp,rgjd->pgd', probs, m_heads)
        d_key = jnp.einsum('rgjp,rgjd->pgd', d_scores, q_heads) * scale
        d_query = d_query + jnp.einsum('rgjp,pgd->rgjd', d_scores, key_tile)
        return d_query, (d_key.astype(jnp.bfloat16), d_value.astype(jnp.bfloat16))

    start = jnp.zeros((ROWS, KVH, group, DH), jnp.float32)
    d_query, outs = lax.scan(step, start, (key_tiles, value_tiles))
    d_queries = (d_query * scale).reshape(ROWS, HQ * DH).astype(jnp.bfloat16)
    d_keys = outs[0].reshape(PROMPT, KVH * DH)
    d_values = outs[1].reshape(PROMPT, KVH * DH)
    return d_queries, d_keys, d_values
```

```python
import functools
import math

import jax
import jax.numpy as jnp
from jax import lax
from jax.experimental import pallas as pl
from jax.experimental.pallas import tpu as pltpu
from jax.sharding import PartitionSpec as P

DH = 128
CORES = 2
RING = 8
SLOTS = 12
TILE = 1024
LOG2E = math.log2(math.e)
MESH = pl.DeviceIdType.MESH
F32 = jnp.float32
BF16 = jnp.bfloat16
NT = (((1,), (1,)), ((), ()))
TN = (((0,), (0,)), ((), ()))


def kernel(
    nx, ny, nz, slots, tile,
    len_ref, q_ref, m_ref, o_ref, lse_ref, k_hbm, v_hbm,
    dq_ref, dk_hbm, dv_hbm,
    k_ref, v_ref, dk_acc, dv_acc, dk_out, dv_out,
    send_rows, send_stats, recv_rows, recv_stats,
    rows_all, stats_all,
    q_step, m_step, stat_step, dq_acc,
    part_own, part_send, part_recv, z_send, z_recv, reduced, back_send, back_recv,
    local_sem,
    xy_send, xy_recv, xys_send, xys_recv,
    ring_send, ring_recv, rings_send, rings_recv,
    sib_send, sib_recv, sibs_send, sibs_recv,
    part_ssem, part_rsem, z_ssem, z_rsem, back_ssem, back_rsem,
):
    x = lax.axis_index("head")
    c = lax.axis_index("ctx")
    core = lax.rem(c, CORES)
    z = lax.rem(lax.div(c, CORES), nz)
    y = lax.div(c, CORES * nz)
    other = 1 - core
    half = nz // 2
    ctx_len = k_ref.shape[0]
    unit = slots * 8
    scale = 1.0 / DH**0.5

    def device(x_to, y_to, z_to, core_to):
        return (x_to, (y_to * nz + z_to) * CORES + core_to)

    def at_z(offset):
        return lax.rem(z + offset + 2 * nz, nz)

    xy_offsets = [(dx, dy) for dx in range(nx) for dy in range(ny) if (dx, dy) != (0, 0)]

    def xy_to(dx, dy):
        return lax.rem(x + dx, nx), lax.rem(y + dy, ny)

    def xy_from(dx, dy):
        return lax.rem(x - dx + nx, nx), lax.rem(y - dy + ny, ny)

    load_k = pltpu.make_async_copy(k_hbm, k_ref, local_sem.at[0])
    load_v = pltpu.make_async_copy(v_hbm, v_ref, local_sem.at[1])
    load_k.start()
    load_v.start()

    barrier = pltpu.get_barrier_semaphore()
    partners = [device(*xy_to(dx, dy), z, core) for dx, dy in xy_offsets]
    partners += [device(x, y, at_z(dz), core) for dz in range(1, nz)]
    partners += [device(x, y, z, other)]
    for partner in partners:
        pl.semaphore_signal(barrier, inc=1, device_id=partner, device_id_type=MESH)

    heads = nx * 16
    row = lax.broadcasted_iota(jnp.int32, (heads, 128), 0)
    lane = lax.broadcasted_iota(jnp.int32, (heads, 128), 1)
    delta = jnp.sum(m_ref[...].astype(F32) * o_ref[...].astype(F32), axis=1, keepdims=True)
    lse_row = lse_ref[...].astype(F32) * LOG2E
    square_row = lax.broadcasted_iota(jnp.int32, (heads, heads), 0)
    square_lane = lax.broadcasted_iota(jnp.int32, (heads, heads), 1)
    lse_col = jnp.sum(
        jnp.where(square_row == square_lane, jnp.broadcast_to(lse_row, (heads, heads)), 0.0),
        axis=1, keepdims=True,
    )
    diagonal = lax.rem(lane, 8) == lax.rem(row, 8)

    def along_lanes(column):
        spread = jnp.where(diagonal, jnp.broadcast_to(column, (heads, 128)), 0.0)
        return jnp.sum(spread.reshape(heads // 8, 8, 128), axis=1)

    lse_lanes = along_lanes(lse_col)
    delta_lanes = along_lanes(delta)
    for i in range(nx):
        send_rows[i, 0:16, :] = q_ref[16 * i : 16 * i + 16, :]
        send_rows[i, 16:32, :] = m_ref[16 * i : 16 * i + 16, :]
        send_stats[i, 0:2, :] = lse_lanes[2 * i : 2 * i + 2]
        send_stats[i, 2:4, :] = delta_lanes[2 * i : 2 * i + 2]

    pl.semaphore_wait(barrier, len(partners))

    mine = x * ny + y

    def xy_copies(i, dx, dy):
        x_to, y_to = xy_to(dx, dy)
        to = device(x_to, y_to, z, core)
        return (
            pltpu.make_async_remote_copy(
                src_ref=send_rows.at[x_to], dst_ref=recv_rows.at[mine],
                send_sem=xy_send.at[i], recv_sem=xy_recv.at[i],
                device_id=to, device_id_type=MESH,
            ),
            pltpu.make_async_remote_copy(
                src_ref=send_stats.at[x_to], dst_ref=recv_stats.at[mine],
                send_sem=xys_send.at[i], recv_sem=xys_recv.at[i],
                device_id=to, device_id_type=MESH,
            ),
        )

    pending = []
    for i, (dx, dy) in enumerate(xy_offsets):
        for copy in xy_copies(i, dx, dy):
            copy.start()
            pending.append(copy)
    recv_rows[mine] = send_rows[x]
    recv_stats[mine] = send_stats[x]
    dk_acc[...] = jnp.zeros_like(dk_acc)
    dv_acc[...] = jnp.zeros_like(dv_acc)
    for copy in pending:
        copy.wait_recv()

    stride = nz * CORES
    place = z * CORES + core
    starts, counts = [], []
    total = jnp.int32(0)
    for h in range(nx):
        live = lax.div(len_ref[h] - place + (stride - 1), stride)
        live = jnp.minimum(jnp.maximum(live, 0), ny)
        starts.append(total)
        counts.append(live)
        total = total + live

    stat_lane = lax.broadcasted_iota(jnp.int32, (4, 128), 1)

    def slot_rows(s):
        sample = jnp.int32(0)
        first = jnp.int32(0)
        for h in range(1, nx):
            past = s >= starts[h]
            sample = jnp.where(past, h, sample)
            first = jnp.where(past, starts[h], first)
        valid = s < total
        index = jnp.where(valid, sample * ny + (s - first), 0)
        packet = recv_rows[index].astype(F32).reshape(4, 8, 128)
        packet = jnp.where(valid, packet, 0.0)
        stat = jnp.where(jnp.logical_and(lax.div(stat_lane, 8) == s, valid), recv_stats[index], 0.0)
        return packet, stat

    stats = jnp.zeros((4, 128), F32)
    for s in range(0, slots, 2):
        first, stat = slot_rows(s)
        second, stat_second = slot_rows(s + 1)
        stats = stats + stat + stat_second
        for part in range(2):
            for g in range(2):
                both = jnp.concatenate([first[2 * part + g], second[2 * part + g]], axis=0)
                rows_all[z, core, part, g, 8 * s : 8 * s + 16, :] = both.astype(BF16)
    stats_all[z, core] = stats

    def ring_copies(direction, hop):
        step = 1 if direction == 0 else -1
        block = at_z(-step * (hop - 1))
        to = device(x, y, at_z(step), core)
        return (
            pltpu.make_async_remote_copy(
                src_ref=rows_all.at[block, core], dst_ref=rows_all.at[block, core],
                send_sem=ring_send.at[direction, hop], recv_sem=ring_recv.at[direction, hop],
                device_id=to, device_id_type=MESH,
            ),
            pltpu.make_async_remote_copy(
                src_ref=stats_all.at[block, core], dst_ref=stats_all.at[block, core],
                send_sem=rings_send.at[direction, hop], recv_sem=rings_recv.at[direction, hop],
                device_id=to, device_id_type=MESH,
            ),
        )

    def ring_arrived(direction, hop):
        step = 1 if direction == 0 else -1
        block = at_z(-step * hop)
        to = device(x, y, at_z(step), core)
        pltpu.make_async_remote_copy(
            src_ref=rows_all.at[block, core], dst_ref=rows_all.at[block, core],
            send_sem=ring_send.at[direction, hop], recv_sem=ring_recv.at[direction, hop],
            device_id=to, device_id_type=MESH,
        ).wait_recv()
        pltpu.make_async_remote_copy(
            src_ref=stats_all.at[block, core], dst_ref=stats_all.at[block, core],
            send_sem=rings_send.at[direction, hop], recv_sem=rings_recv.at[direction, hop],
            device_id=to, device_id_type=MESH,
        ).wait_recv()

    def sibling_copies(offset, side):
        block = at_z(offset)
        return (
            pltpu.make_async_remote_copy(
                src_ref=rows_all.at[block, side], dst_ref=rows_all.at[block, side],
                send_sem=sib_send.at[offset], recv_sem=sib_recv.at[offset],
                device_id=device(x, y, z, other), device_id_type=MESH,
            ),
            pltpu.make_async_remote_copy(
                src_ref=stats_all.at[block, side], dst_ref=stats_all.at[block, side],
                send_sem=sibs_send.at[offset], recv_sem=sibs_recv.at[offset],
                device_id=device(x, y, z, other), device_id_type=MESH,
            ),
        )

    def start(copies):
        for copy in copies:
            copy.start()

    def advance(hop):
        ring_arrived(0, hop)
        if isinstance(hop, int):
            if hop < half:
                start(ring_copies(0, hop + 1))
        else:
            start(ring_copies(0, hop + 1))
        start(sibling_copies(nz - hop, core))
        if not isinstance(hop, int) or hop < half:
            ring_arrived(1, hop)
            if isinstance(hop, int):
                if hop + 1 < half:
                    start(ring_copies(1, hop + 1))
            else:

                @pl.when(hop + 1 < half)
                def _():
                    start(ring_copies(1, hop + 1))

            start(sibling_copies(hop, core))

    def sibling_arrived(offset):
        for copy in sibling_copies(offset, other):
            copy.wait_recv()

    def gather_step(offsets):
        count = 2 * len(offsets)
        width = unit * count
        pieces = []
        for n, offset in enumerate(offsets):
            for side, which in enumerate((core, other)):
                at = (2 * n + side) * unit
                for g in range(2):
                    q_step[g, at : at + unit, :] = rows_all[at_z(offset), which, 0, g]
                    m_step[g, at : at + unit, :] = rows_all[at_z(offset), which, 1, g]
                pieces.append(stats_all[at_z(offset), which][:, :unit])
        joined = jnp.concatenate(pieces, axis=1) if count > 1 else pieces[0]
        stat_step[:, 0:width] = joined
        dq_acc[:, 0:width, :] = jnp.zeros((2, width, 128), F32)
        return width

    def compute(width, index):
        here = pl.ds(pl.multiple_of(index * tile, tile), tile)
        for g in range(2):
            cols = slice(g * DH, (g + 1) * DH)
            q = q_step[g, 0:width, :]
            m = m_step[g, 0:width, :]
            lse = stat_step[g : g + 1, 0:width]
            dlt = stat_step[2 + g : 3 + g, 0:width]
            k = k_ref[here, cols]
            v = v_ref[here, cols]
            scores = lax.dot_general(k, q, NT, preferred_element_type=F32)
            d_weights = lax.dot_general(v, m, NT, preferred_element_type=F32)
            weights = jnp.exp2(scores * (scale * LOG2E) - lse)
            d_scores = (weights * (d_weights - dlt)).astype(BF16)
            probs = weights.astype(BF16)
            dv_acc[here, cols] += jnp.dot(probs, m, preferred_element_type=F32)
            dk_acc[here, cols] += jnp.dot(d_scores, q, preferred_element_type=F32)
            dq_acc[g, 0:width, :] += lax.dot_general(d_scores, k, TN, preferred_element_type=F32)

    def part_copy(offset):
        return pltpu.make_async_remote_copy(
            src_ref=part_send.at[offset], dst_ref=part_recv.at[offset],
            send_sem=part_ssem.at[offset], recv_sem=part_rsem.at[offset],
            device_id=device(x, y, z, other), device_id_type=MESH,
        )

    def z_copy(offset):
        return pltpu.make_async_remote_copy(
            src_ref=z_send.at[offset], dst_ref=z_recv.at[offset],
            send_sem=z_ssem.at[offset], recv_sem=z_rsem.at[offset],
            device_id=device(x, y, at_z(offset), core), device_id_type=MESH,
        )

    def give_parts(offsets):
        for n, offset in enumerate(offsets):
            at = 2 * n * unit
            for g in range(2):
                part_own[offset, g] = dq_acc[g, at : at + unit, :]
                part_send[offset, g] = dq_acc[g, at + unit : at + 2 * unit, :].astype(BF16)
            part_copy(offset).start()

    def pass_parts(offsets):
        for offset in offsets:
            part_copy(offset).wait_recv()
            z_send[offset] = (part_own[offset] + part_recv[offset].astype(F32)).astype(BF16)
            z_copy(offset).start()

    tiles = ctx_len // tile
    early = tiles // 2

    def run_tiles(width, low, high):
        lax.fori_loop(low, high, lambda i, carry: (compute(width, i), carry)[1], 0)

    start(ring_copies(0, 1))
    if half > 1:
        start(ring_copies(1, 1))
    start(sibling_copies(0, core))
    load_k.wait()
    load_v.wait()
    sibling_arrived(0)
    width = gather_step([0])
    run_tiles(width, 0, early)
    advance(1)
    run_tiles(width, early, tiles)
    give_parts([0])

    def middle(hop, carry):
        sibling_arrived(hop)
        sibling_arrived(nz - hop)
        wide = gather_step([hop, nz - hop])

        def turn(part, inner):
            @pl.when(part == 1)
            def _():
                @pl.when(hop + 1 < half)
                def _():
                    advance(hop + 1)

                @pl.when(hop + 1 == half)
                def _():
                    advance(half)

                @pl.when(hop > 1)
                def _():
                    pass_parts([hop - 1, nz - hop + 1])

            run_tiles(wide, part * early, part * early + early)
            return inner

        lax.fori_loop(0, 2, turn, 0)
        give_parts([hop, nz - hop])
        return carry

    lax.fori_loop(1, half, middle, 0)

    sibling_arrived(half)
    width = gather_step([half])
    run_tiles(width, 0, early)
    if half > 1:
        pass_parts([half - 1, half + 1])
    run_tiles(width, early, tiles)
    give_parts([half])

    dv_out[...] = dv_acc[...].astype(BF16)
    store_v = pltpu.make_async_copy(dv_out, dv_hbm, local_sem.at[0])
    store_v.start()
    pass_parts([half])
    dk_out[...] = (dk_acc[...] * scale).astype(BF16)
    store_k = pltpu.make_async_copy(dk_out, dk_hbm, local_sem.at[1])
    store_k.start()

    part_copy(0).wait_recv()
    result = part_own[0] + part_recv[0].astype(F32)
    for offset in range(1, nz):
        z_copy(offset).wait_recv()
        result = result + z_recv[offset].astype(F32)
    for g in range(2):
        reduced[:, 8 * g : 8 * g + 8, :] = result[g].reshape(slots, 8, 128)

    for h in range(nx):
        for row_y in range(ny):
            valid = row_y < counts[h]
            slot = jnp.where(valid, starts[h] + row_y, 0)
            back_send[h * ny + row_y] = jnp.where(valid, reduced[slot], 0.0).astype(BF16)

    def back_copy(i, dx, dy):
        x_to, y_to = xy_to(dx, dy)
        return pltpu.make_async_remote_copy(
            src_ref=back_send.at[x_to * ny + y_to], dst_ref=back_recv.at[mine],
            send_sem=back_ssem.at[i], recv_sem=back_rsem.at[i],
            device_id=device(x_to, y_to, z, core), device_id_type=MESH,
        )

    backs = [back_copy(i, dx, dy) for i, (dx, dy) in enumerate(xy_offsets)]
    start(backs)
    back_recv[mine] = back_send[mine]
    for copy in backs:
        copy.wait_recv()
    for i in range(nx):
        owned = back_recv[i * ny].astype(F32)
        for row_y in range(1, ny):
            owned = owned + back_recv[i * ny + row_y].astype(F32)
        dq_ref[16 * i : 16 * i + 16, :] = (owned * scale).astype(BF16)

    for copy in pending + backs:
        copy.wait_send()
    for hop in range(1, half + 1):
        for copy in ring_copies(0, hop):
            copy.wait_send()
        if hop < half:
            for copy in ring_copies(1, hop):
                copy.wait_send()
    for offset in range(nz):
        for copy in sibling_copies(offset, core):
            copy.wait_send()
        part_copy(offset).wait_send()
        if offset > 0:
            z_copy(offset).wait_send()
    store_v.wait()
    store_k.wait()


def fused(nx, ny, nz, slots, tile, lengths, q, m, o, lse, keys, values):
    ctx_len, kv_cols = keys.shape
    unit = slots * 8
    widest = 4 * unit
    vmem = pl.BlockSpec(memory_space=pltpu.VMEM)
    smem = pl.BlockSpec(memory_space=pltpu.SMEM)
    hbm = pl.BlockSpec(memory_space=pl.ANY)
    dma = pltpu.SemaphoreType.DMA
    packets = nx * ny
    half = nz // 2
    scratch = [
        pltpu.VMEM((ctx_len, kv_cols), BF16),
        pltpu.VMEM((ctx_len, kv_cols), BF16),
        pltpu.VMEM((ctx_len, kv_cols), F32),
        pltpu.VMEM((ctx_len, kv_cols), F32),
        pltpu.VMEM((ctx_len, kv_cols), BF16),
        pltpu.VMEM((ctx_len, kv_cols), BF16),
        pltpu.VMEM((nx, 32, 128), BF16),
        pltpu.VMEM((nx, 4, 128), F32),
        pltpu.VMEM((packets, 32, 128), BF16),
        pltpu.VMEM((packets, 4, 128), F32),
        pltpu.VMEM((nz, CORES, 2, 2, unit, 128), BF16),
        pltpu.VMEM((nz, CORES, 4, 128), F32),
        pltpu.VMEM((2, widest, 128), BF16),
        pltpu.VMEM((2, widest, 128), BF16),
        pltpu.VMEM((4, widest), F32),
        pltpu.VMEM((2, widest, 128), F32),
        pltpu.VMEM((nz, 2, unit, 128), F32),
        pltpu.VMEM((nz, 2, unit, 128), BF16),
        pltpu.VMEM((nz, 2, unit, 128), BF16),
        pltpu.VMEM((nz, 2, unit, 128), BF16),
        pltpu.VMEM((nz, 2, unit, 128), BF16),
        pltpu.VMEM((slots, 16, 128), F32),
        pltpu.VMEM((packets, 16, 128), BF16),
        pltpu.VMEM((packets, 16, 128), BF16),
        dma((2,)),
        dma((packets,)), dma((packets,)), dma((packets,)), dma((packets,)),
        dma((2, half + 1)), dma((2, half + 1)), dma((2, half + 1)), dma((2, half + 1)),
        dma((nz,)), dma((nz,)), dma((nz,)), dma((nz,)),
        dma((nz,)), dma((nz,)), dma((nz,)), dma((nz,)),
        dma((packets,)), dma((packets,)),
    ]
    flops = 5 * 2 * ctx_len * 128 * 2 * unit * 2 * nz
    return pl.pallas_call(
        functools.partial(kernel, nx, ny, nz, slots, tile),
        out_shape=(
            jax.ShapeDtypeStruct(q.shape, BF16),
            jax.ShapeDtypeStruct(keys.shape, BF16),
            jax.ShapeDtypeStruct(values.shape, BF16),
        ),
        in_specs=[smem, vmem, vmem, vmem, vmem, hbm, hbm],
        out_specs=(vmem, hbm, hbm),
        scratch_shapes=scratch,
        compiler_params=pltpu.CompilerParams(
            collective_id=0, has_side_effects=True, vmem_limit_bytes=56 << 20
        ),
        cost_estimate=pl.CostEstimate(
            flops=flops, bytes_accessed=8 * ctx_len * kv_cols, transcendentals=0
        ),
    )(lengths, q, m, o, lse, keys, values)


def solution(mesh, nz=RING, slots=SLOTS, tile=TILE):
    nx = mesh.shape["head"]
    ny = mesh.shape["ctx"] // (nz * CORES)

    def on_device(queries, d_out, out_rows, lse, lengths, keys, values):
        heads = queries.shape[1] // DH
        d_q, d_k, d_v = fused(
            nx, ny, nz, slots, tile, lengths,
            queries.reshape(heads, DH), d_out.reshape(heads, DH), out_rows.reshape(heads, DH),
            lse, keys, values,
        )
        return d_q.reshape(1, heads * DH), d_k, d_v

    rows = P(("head", "ctx"), None)
    return jax.shard_map(
        on_device,
        mesh=mesh,
        in_specs=(rows, rows, rows, rows, P(), P("ctx", "head"), P("ctx", "head")),
        out_specs=(rows, P("ctx", "head"), P("ctx", "head")),
        check_vma=False,
    )
```

```python
import functools
import math

import jax
import jax.numpy as jnp
from jax import lax
from jax.experimental import pallas as pl
from jax.experimental.pallas import tpu as pltpu
from jax.sharding import PartitionSpec as P

DH = 128
CORES = 2
RING = 8
SLOTS = 12
TILE = 256
LOG2E = math.log2(math.e)
PIECES = 4
MESH = pl.DeviceIdType.MESH
F32 = jnp.float32
BF16 = jnp.bfloat16
NT = (((1,), (1,)), ((), ()))
TN = (((0,), (0,)), ((), ()))


def kernel(
    nx, ny, nz, slots, tile,
    len_ref, q_ref, m_ref, o_ref, lse_ref, k_hbm, v_hbm,
    dq_ref, dk_hbm, dv_hbm,
    k_ref, v_ref, dk_out, dv_out,
    send_rows, send_stats, recv_rows, recv_stats,
    rows_all, stats_all,
    q_all, m_all, stat_all, probs, d_scores,
    part_own, part_send, part_recv, z_send, z_recv, reduced, back_send, back_recv,
    load_sem, store_sem,
    xy_send, xy_recv, xys_send, xys_recv,
    ring_send, ring_recv, rings_send, rings_recv,
    sib_send, sib_recv, sibs_send, sibs_recv,
    part_ssem, part_rsem, z_ssem, z_rsem, back_ssem, back_rsem,
):
    x = lax.axis_index("head")
    c = lax.axis_index("ctx")
    core = lax.rem(c, CORES)
    z = lax.rem(lax.div(c, CORES), nz)
    y = lax.div(c, CORES * nz)
    other = 1 - core
    half = nz // 2
    ctx_len = k_ref.shape[0]
    unit = slots * 8
    scale = 1.0 / DH**0.5

    def device(x_to, y_to, z_to, core_to):
        return (x_to, (y_to * nz + z_to) * CORES + core_to)

    def at_z(offset):
        return lax.rem(z + offset + 2 * nz, nz)

    xy_offsets = [(dx, dy) for dx in range(nx) for dy in range(ny) if (dx, dy) != (0, 0)]

    def xy_to(dx, dy):
        return lax.rem(x + dx, nx), lax.rem(y + dy, ny)

    def xy_from(dx, dy):
        return lax.rem(x - dx + nx, nx), lax.rem(y - dy + ny, ny)

    load_k = pltpu.make_async_copy(k_hbm, k_ref, load_sem.at[0])
    load_v = pltpu.make_async_copy(v_hbm, v_ref, load_sem.at[1])
    load_k.start()
    load_v.start()

    barrier = pltpu.get_barrier_semaphore()
    partners = [device(*xy_to(dx, dy), z, core) for dx, dy in xy_offsets]
    partners += [device(x, y, at_z(dz), core) for dz in sorted({1, nz - 1})]
    partners += [device(x, y, z, other)]
    for partner in partners:
        pl.semaphore_signal(barrier, inc=1, device_id=partner, device_id_type=MESH)

    heads = nx * 16
    row = lax.broadcasted_iota(jnp.int32, (heads, 128), 0)
    lane = lax.broadcasted_iota(jnp.int32, (heads, 128), 1)
    q_heads = q_ref[...].astype(F32).reshape(heads, DH)
    m_heads = m_ref[...].astype(F32).reshape(heads, DH)
    o_heads = o_ref[...].astype(F32).reshape(heads, DH)
    delta = jnp.sum(m_heads * o_heads, axis=1, keepdims=True)
    lse_row = lse_ref[...].astype(F32) * LOG2E
    square_row = lax.broadcasted_iota(jnp.int32, (heads, heads), 0)
    square_lane = lax.broadcasted_iota(jnp.int32, (heads, heads), 1)
    lse_col = jnp.sum(
        jnp.where(square_row == square_lane, jnp.broadcast_to(lse_row, (heads, heads)), 0.0),
        axis=1, keepdims=True,
    )
    diagonal = lax.rem(lane, 8) == lax.rem(row, 8)

    def along_lanes(column):
        spread = jnp.where(diagonal, jnp.broadcast_to(column, (heads, 128)), 0.0)
        return jnp.sum(spread.reshape(heads // 8, 8, 128), axis=1)

    lse_lanes = along_lanes(lse_col)
    delta_lanes = along_lanes(delta)
    for i in range(nx):
        send_rows[i, 0:16, :] = q_heads[16 * i : 16 * i + 16].astype(BF16)
        send_rows[i, 16:32, :] = m_heads[16 * i : 16 * i + 16].astype(BF16)
        send_stats[i, 0:2, :] = lse_lanes[2 * i : 2 * i + 2]
        send_stats[i, 2:4, :] = delta_lanes[2 * i : 2 * i + 2]

    pl.semaphore_wait(barrier, len(partners))

    mine = x * ny + y

    def xy_copies(i, dx, dy):
        x_to, y_to = xy_to(dx, dy)
        to = device(x_to, y_to, z, core)
        return (
            pltpu.make_async_remote_copy(
                src_ref=send_rows.at[x_to], dst_ref=recv_rows.at[mine],
                send_sem=xy_send.at[i], recv_sem=xy_recv.at[i],
                device_id=to, device_id_type=MESH,
            ),
            pltpu.make_async_remote_copy(
                src_ref=send_stats.at[x_to], dst_ref=recv_stats.at[mine],
                send_sem=xys_send.at[i], recv_sem=xys_recv.at[i],
                device_id=to, device_id_type=MESH,
            ),
        )

    pending = []
    for i, (dx, dy) in enumerate(xy_offsets):
        for copy in xy_copies(i, dx, dy):
            copy.start()
            pending.append(copy)
    recv_rows[mine] = send_rows[x]
    recv_stats[mine] = send_stats[x]
    for copy in pending:
        copy.wait_recv()

    stride = nz * CORES
    place = z * CORES + core
    starts, counts = [], []
    total = jnp.int32(0)
    for h in range(nx):
        live = lax.div(len_ref[h] - place + (stride - 1), stride)
        live = jnp.minimum(jnp.maximum(live, 0), ny)
        starts.append(total)
        counts.append(live)
        total = total + live

    stat_lane = lax.broadcasted_iota(jnp.int32, (4, 128), 1)

    def slot_rows(s):
        sample = jnp.int32(0)
        first = jnp.int32(0)
        for h in range(1, nx):
            past = s >= starts[h]
            sample = jnp.where(past, h, sample)
            first = jnp.where(past, starts[h], first)
        valid = s < total
        index = jnp.where(valid, sample * ny + (s - first), 0)
        packet = recv_rows[index].astype(F32).reshape(4, 8, 128)
        packet = jnp.where(valid, packet, 0.0)
        stat = jnp.where(jnp.logical_and(lax.div(stat_lane, 8) == s, valid), recv_stats[index], 0.0)
        return packet, stat

    stats = jnp.zeros((4, 128), F32)
    for s in range(0, slots, 2):
        first, stat = slot_rows(s)
        second, stat_second = slot_rows(s + 1)
        stats = stats + stat + stat_second
        for part in range(2):
            for g in range(2):
                both = jnp.concatenate([first[2 * part + g], second[2 * part + g]], axis=0)
                rows_all[z, core, part, g, 8 * s : 8 * s + 16, :] = both.astype(BF16)
    stats_all[z, core] = stats

    def when(condition, action):
        if isinstance(condition, bool):
            if condition:
                action()
        else:
            pl.when(condition)(action)

    def start(copies):
        for copy in copies:
            copy.start()

    def chunk_copies(block, side, part, to, sems):
        send, recv, stat_send, stat_recv, index = sems
        copies = [
            pltpu.make_async_remote_copy(
                src_ref=rows_all.at[block, side, part], dst_ref=rows_all.at[block, side, part],
                send_sem=send.at[index + (part,)], recv_sem=recv.at[index + (part,)],
                device_id=to, device_id_type=MESH,
            )
        ]
        if part == 0:
            copies.append(
                pltpu.make_async_remote_copy(
                    src_ref=stats_all.at[block, side], dst_ref=stats_all.at[block, side],
                    send_sem=stat_send.at[index], recv_sem=stat_recv.at[index],
                    device_id=to, device_id_type=MESH,
                )
            )
        return copies

    def ring_copies(direction, hop, part, arriving=False):
        step = 1 if direction == 0 else -1
        block = at_z(-step * (hop if arriving else hop - 1))
        to = device(x, y, at_z(step), core)
        sems = (ring_send, ring_recv, rings_send, rings_recv, (direction, hop))
        return chunk_copies(block, core, part, to, sems)

    def sibling_copies(offset, side, part):
        sems = (sib_send, sib_recv, sibs_send, sibs_recv, (offset,))
        return chunk_copies(at_z(offset), side, part, device(x, y, z, other), sems)

    def advance(part, hop):
        for copy in ring_copies(0, hop, part, arriving=True):
            copy.wait_recv()
        when(hop < half, lambda: start(ring_copies(0, hop + 1, part)))
        start(sibling_copies(nz - hop, core, part))

        def leftward():
            for copy in ring_copies(1, hop, part, arriving=True):
                copy.wait_recv()
            when(hop + 1 < half, lambda: start(ring_copies(1, hop + 1, part)))
            start(sibling_copies(hop, core, part))

        when(hop < half, leftward)

    middle_width = 4 * unit
    own_at = (half - 1) * middle_width
    far_at = own_at + 2 * unit
    columns = far_at + 2 * unit
    far_from = far_at // 128 * 128

    def gather(offsets, at):
        for part, held in enumerate((q_all, m_all)):
            for offset in offsets:
                for copy in sibling_copies(offset, other, part):
                    copy.wait_recv()
            for n, offset in enumerate(offsets):
                for side, which in enumerate((core, other)):
                    for g in range(2):
                        to = at + (2 * n + side) * unit
                        if not isinstance(to, int):
                            to = pl.multiple_of(to, 16)
                        held[g, pl.ds(to, unit), :] = rows_all[at_z(offset), which, part, g]

    def stat_lanes(offsets):
        pieces = [
            stats_all[at_z(offset), which][:, :unit]
            for offset in offsets for which in (core, other)
        ]
        return jnp.concatenate(pieces, axis=1)

    def front(at, width, g):
        if isinstance(at, int):
            cols = slice(at, at + width)
        else:
            cols = pl.ds(pl.multiple_of(at, 128), width)
        rows = pl.ds(at if isinstance(at, int) else pl.multiple_of(at, 128), width)
        dims = slice(g * DH, (g + 1) * DH)
        k = k_ref[:, dims]
        scores = lax.dot_general(k, q_all[g, rows, :], NT, preferred_element_type=F32)
        weights = jnp.exp2(scores * (scale * LOG2E) - stat_all[g : g + 1, cols])
        probs[g, :, cols] = weights.astype(BF16)
        d_weights = lax.dot_general(
            v_ref[:, dims], m_all[g, rows, :], NT, preferred_element_type=F32
        )
        d_score = (weights * (d_weights - stat_all[2 + g : 3 + g, cols])).astype(BF16)
        d_scores[g, :, cols] = d_score
        return lax.dot_general(d_score, k, TN, preferred_element_type=F32)

    def back(index):
        here = pl.ds(pl.multiple_of(index * tile, tile), tile)
        for g in range(2):
            dims = slice(g * DH, (g + 1) * DH)
            d_v = jnp.dot(probs[g, here, :], m_all[g], preferred_element_type=F32)
            dv_out[here, dims] = d_v.astype(BF16)
            d_k = jnp.dot(d_scores[g, here, :], q_all[g], preferred_element_type=F32)
            dk_out[here, dims] = (d_k * scale).astype(BF16)

    def part_copy(offset):
        return pltpu.make_async_remote_copy(
            src_ref=part_send.at[offset], dst_ref=part_recv.at[offset],
            send_sem=part_ssem.at[offset], recv_sem=part_rsem.at[offset],
            device_id=device(x, y, z, other), device_id_type=MESH,
        )

    def z_copy(offset):
        return pltpu.make_async_remote_copy(
            src_ref=z_send.at[offset], dst_ref=z_recv.at[offset],
            send_sem=z_ssem.at[offset], recv_sem=z_rsem.at[offset],
            device_id=device(x, y, at_z(offset), core), device_id_type=MESH,
        )

    def keep_parts(offsets, g, d_query):
        for n, offset in enumerate(offsets):
            at = 2 * n * unit
            part_own[offset, g] = d_query[at : at + unit]
            part_send[offset, g] = d_query[at + unit : at + 2 * unit].astype(BF16)

    def give_parts(offsets):
        for offset in offsets:
            part_copy(offset).start()

    def pass_parts(offsets):
        for offset in offsets:
            part_copy(offset).wait_recv()
            z_send[offset] = (part_own[offset] + part_recv[offset].astype(F32)).astype(BF16)
            z_copy(offset).start()

    for part in range(2):
        start(ring_copies(0, 1, part))
        if half > 1:
            start(ring_copies(1, 1, part))
        start(sibling_copies(0, core, part))
    load_k.wait()
    load_v.wait()
    gather([0], own_at)
    stat_all[:, own_at:far_at] = stat_lanes([0])
    for g in range(2):
        keep_parts([0], g, front(own_at, far_at - own_at, g))
    give_parts([0])
    advance(0, 1)

    def middle(hop, carry):
        offsets = [hop, nz - hop]
        at = (hop - 1) * middle_width
        advance(1, hop)
        gather(offsets, at)
        stat_all[:, pl.ds(pl.multiple_of(at, 128), middle_width)] = stat_lanes(offsets)
        keep_parts(offsets, 0, front(at, middle_width, 0))
        advance(0, hop + 1)

        @pl.when(hop > 1)
        def _():
            pass_parts([hop - 1, nz - hop + 1])

        keep_parts(offsets, 1, front(at, middle_width, 1))
        give_parts(offsets)
        return carry

    lax.fori_loop(1, half, middle, 0)

    advance(1, half)
    gather([half], far_at)
    stat_all[:, own_at:columns] = stat_lanes([0, half])
    for g in range(2):
        d_query = front(far_from, columns - far_from, g)
        keep_parts([half], g, d_query[far_at - far_from :])
        if g == 0 and half > 1:
            pass_parts([half - 1, half + 1])
    give_parts([half])

    tiles = ctx_len // tile

    def stores(index):
        here = pl.ds(pl.multiple_of(index * tile, tile), tile)
        return (
            pltpu.make_async_copy(dv_out.at[here], dv_hbm.at[here], store_sem.at[0, index]),
            pltpu.make_async_copy(dk_out.at[here], dk_hbm.at[here], store_sem.at[1, index]),
        )

    def finish_tiles(low, high):
        def one(index, carry):
            back(index)
            start(stores(index))
            return carry

        lax.fori_loop(low, high, one, 0)

    first, last = tiles // 8, tiles - tiles // 8
    finish_tiles(0, first)
    pass_parts([half])
    finish_tiles(first, last)

    part_copy(0).wait_recv()
    result = part_own[0] + part_recv[0].astype(F32)
    for offset in range(1, nz):
        z_copy(offset).wait_recv()
        result = result + z_recv[offset].astype(F32)
    for g in range(2):
        reduced[:, 8 * g : 8 * g + 8, :] = result[g].reshape(slots, 8, 128)

    for h in range(nx):
        for row_y in range(ny):
            valid = row_y < counts[h]
            slot = jnp.where(valid, starts[h] + row_y, 0)
            back_send[h * ny + row_y] = jnp.where(valid, reduced[slot], 0.0).astype(BF16)

    def back_copy(i, dx, dy):
        x_to, y_to = xy_to(dx, dy)
        return pltpu.make_async_remote_copy(
            src_ref=back_send.at[x_to * ny + y_to], dst_ref=back_recv.at[mine],
            send_sem=back_ssem.at[i], recv_sem=back_rsem.at[i],
            device_id=device(x_to, y_to, z, core), device_id_type=MESH,
        )

    backs = [back_copy(i, dx, dy) for i, (dx, dy) in enumerate(xy_offsets)]
    start(backs)
    back_recv[mine] = back_send[mine]
    finish_tiles(last, tiles)
    for copy in backs:
        copy.wait_recv()
    for i in range(nx):
        owned = back_recv[i * ny].astype(F32)
        for row_y in range(1, ny):
            owned = owned + back_recv[i * ny + row_y].astype(F32)
        dq_ref[:, 16 * DH * i : 16 * DH * (i + 1)] = (owned * scale).reshape(1, 16 * DH).astype(BF16)

    for copy in pending + backs:
        copy.wait_send()
    for part in range(2):
        for hop in range(1, half + 1):
            for copy in ring_copies(0, hop, part):
                copy.wait_send()
            if hop < half:
                for copy in ring_copies(1, hop, part):
                    copy.wait_send()
        for offset in range(nz):
            for copy in sibling_copies(offset, core, part):
                copy.wait_send()
    for offset in range(nz):
        part_copy(offset).wait_send()
        if offset > 0:
            z_copy(offset).wait_send()

    def stored(index, carry):
        for copy in stores(index):
            copy.wait()
        return carry

    lax.fori_loop(0, tiles, stored, 0)


def fused(nx, ny, nz, slots, tile, lengths, q, m, o, lse, keys, values):
    ctx_len, kv_cols = keys.shape
    unit = slots * 8
    columns = 2 * nz * unit
    vmem = pl.BlockSpec(memory_space=pltpu.VMEM)
    smem = pl.BlockSpec(memory_space=pltpu.SMEM)
    hbm = pl.BlockSpec(memory_space=pl.ANY)
    dma = pltpu.SemaphoreType.DMA
    packets = nx * ny
    half = nz // 2
    scratch = [
        pltpu.VMEM((ctx_len, kv_cols), BF16),
        pltpu.VMEM((ctx_len, kv_cols), BF16),
        pltpu.VMEM((ctx_len, kv_cols), BF16),
        pltpu.VMEM((ctx_len, kv_cols), BF16),
        pltpu.VMEM((nx, 32, 128), BF16),
        pltpu.VMEM((nx, 4, 128), F32),
        pltpu.VMEM((packets, 32, 128), BF16),
        pltpu.VMEM((packets, 4, 128), F32),
        pltpu.VMEM((nz, CORES, 2, 2, unit, 128), BF16),
        pltpu.VMEM((nz, CORES, 4, 128), F32),
        pltpu.VMEM((2, columns, 128), BF16),
        pltpu.VMEM((2, columns, 128), BF16),
        pltpu.VMEM((4, columns), F32),
        pltpu.VMEM((2, ctx_len, columns), BF16),
        pltpu.VMEM((2, ctx_len, columns), BF16),
        pltpu.VMEM((nz, 2, unit, 128), F32),
        pltpu.VMEM((nz, 2, unit, 128), BF16),
        pltpu.VMEM((nz, 2, unit, 128), BF16),
        pltpu.VMEM((nz, 2, unit, 128), BF16),
        pltpu.VMEM((nz, 2, unit, 128), BF16),
        pltpu.VMEM((slots, 16, 128), F32),
        pltpu.VMEM((packets, 16, 128), BF16),
        pltpu.VMEM((packets, 16, 128), BF16),
        dma((2,)), dma((2, ctx_len // tile)),
        dma((packets,)), dma((packets,)), dma((packets,)), dma((packets,)),
        dma((2, half + 1, 2)), dma((2, half + 1, 2)), dma((2, half + 1)), dma((2, half + 1)),
        dma((nz, 2)), dma((nz, 2)), dma((nz,)), dma((nz,)),
        dma((nz,)), dma((nz,)), dma((nz,)), dma((nz,)),
        dma((packets,)), dma((packets,)),
    ]
    flops = 5 * 2 * ctx_len * 128 * 2 * unit * 2 * nz
    return pl.pallas_call(
        functools.partial(kernel, nx, ny, nz, slots, tile),
        out_shape=(
            jax.ShapeDtypeStruct(q.shape, BF16),
            jax.ShapeDtypeStruct(keys.shape, BF16),
            jax.ShapeDtypeStruct(values.shape, BF16),
        ),
        in_specs=[smem, vmem, vmem, vmem, vmem, hbm, hbm],
        out_specs=(vmem, hbm, hbm),
        scratch_shapes=scratch,
        compiler_params=pltpu.CompilerParams(
            collective_id=0, has_side_effects=True, vmem_limit_bytes=56 << 20
        ),
        cost_estimate=pl.CostEstimate(
            flops=flops, bytes_accessed=8 * ctx_len * kv_cols, transcendentals=0
        ),
    )(lengths, q, m, o, lse, keys, values)


def hand_over_kernel(dq_in, dk_in, dv_in, dq_out, dk_out, dv_out, dk_held, dv_held, sems):
    pieces = sems.shape[2]
    size = dk_in.shape[0] // pieces
    moves = []
    for i in range(pieces):
        here = pl.ds(i * size, size)
        for n, (source, held, target) in enumerate(
            ((dk_in, dk_held, dk_out), (dv_in, dv_held, dv_out))
        ):
            moves.append((
                pltpu.make_async_copy(source.at[here], held.at[here], sems.at[0, n, i]),
                pltpu.make_async_copy(held.at[here], target.at[here], sems.at[1, n, i]),
            ))
    for load, _ in moves:
        load.start()
    dq_out[...] = dq_in[...]
    for load, store in moves:
        load.wait()
        store.start()
    for _, store in moves:
        store.wait()


def hand_over(d_q, d_k, d_v, pieces=PIECES):
    vmem = pl.BlockSpec(memory_space=pltpu.VMEM)
    hbm = pl.BlockSpec(memory_space=pl.ANY)
    return pl.pallas_call(
        hand_over_kernel,
        out_shape=tuple(jax.ShapeDtypeStruct(a.shape, a.dtype) for a in (d_q, d_k, d_v)),
        in_specs=[vmem, hbm, hbm],
        out_specs=(vmem, hbm, hbm),
        scratch_shapes=[
            pltpu.VMEM(d_k.shape, BF16), pltpu.VMEM(d_v.shape, BF16),
            pltpu.SemaphoreType.DMA((2, 2, pieces)),
        ],
        compiler_params=pltpu.CompilerParams(vmem_limit_bytes=56 << 20),
    )(d_q, d_k, d_v)


def solution(mesh, nz=RING, slots=SLOTS, tile=TILE):
    nx = mesh.shape["head"]
    ny = mesh.shape["ctx"] // (nz * CORES)

    def on_device(queries, d_out, out_rows, lse, lengths, keys, values):
        d_q, d_k, d_v = fused(
            nx, ny, nz, slots, tile, lengths,
            queries, d_out, out_rows, lse, keys, values,
        )
        return hand_over(d_q, d_k, d_v)

    rows = P(("head", "ctx"), None)
    return jax.shard_map(
        on_device,
        mesh=mesh,
        in_specs=(rows, rows, rows, rows, P(), P("ctx", "head"), P("ctx", "head")),
        out_specs=(rows, P("ctx", "head"), P("ctx", "head")),
        check_vma=False,
    )
```

```python
import functools
import math

import jax
import jax.numpy as jnp
from jax import lax
from jax.experimental import pallas as pl
from jax.experimental.pallas import tpu as pltpu
from jax.sharding import PartitionSpec as P

DH = 128
CORES = 2
RING = 8
SLOTS = 12
TILE = 512
LOG2E = math.log2(math.e)
PIECES = 4
MESH = pl.DeviceIdType.MESH
F32 = jnp.float32
BF16 = jnp.bfloat16
NT = (((1,), (1,)), ((), ()))
TN = (((0,), (0,)), ((), ()))


def kernel(
    nx, ny, nz, slots, tile,
    len_ref, q_ref, m_ref, o_ref, lse_ref, k_hbm, v_hbm,
    dq_ref, dk_hbm, dv_hbm,
    k_ref, v_ref, dk_out, dv_out, dk_give, dv_give, dk_got, dv_got,
    send_rows, send_stats, recv_rows, recv_stats,
    rows_all, stats_all,
    q_all, m_all, stat_all, probs, d_scores, dq_half, dq_own,
    z_send, z_recv, reduced, back_send, back_recv,
    load_sem, store_sem, kv_send, kv_recv, give_send, give_recv,
    xy_send, xy_recv, xys_send, xys_recv,
    ring_send, ring_recv, rings_send, rings_recv,
    z_ssem, z_rsem, back_ssem, back_rsem,
):
    x = lax.axis_index("head")
    c = lax.axis_index("ctx")
    core = lax.rem(c, CORES)
    z = lax.rem(lax.div(c, CORES), nz)
    y = lax.div(c, CORES * nz)
    other = 1 - core
    half = nz // 2
    ctx_len = k_ref.shape[1]
    unit = slots * 8
    scale = 1.0 / DH**0.5

    def device(x_to, y_to, z_to, core_to):
        return (x_to, (y_to * nz + z_to) * CORES + core_to)

    def at_z(offset):
        return lax.rem(z + offset + 2 * nz, nz)

    xy_offsets = [(dx, dy) for dx in range(nx) for dy in range(ny) if (dx, dy) != (0, 0)]

    def xy_to(dx, dy):
        return lax.rem(x + dx, nx), lax.rem(y + dy, ny)

    def xy_from(dx, dy):
        return lax.rem(x - dx + nx, nx), lax.rem(y - dy + ny, ny)

    load_k = pltpu.make_async_copy(k_hbm, k_ref.at[0], load_sem.at[0])
    load_v = pltpu.make_async_copy(v_hbm, v_ref.at[0], load_sem.at[1])
    load_k.start()
    load_v.start()

    barrier = pltpu.get_barrier_semaphore()
    partners = [device(*xy_to(dx, dy), z, core) for dx, dy in xy_offsets]
    partners += [device(x, y, at_z(dz), core) for dz in sorted({1, nz - 1})]
    partners += [device(x, y, z, other)]
    for partner in partners:
        pl.semaphore_signal(barrier, inc=1, device_id=partner, device_id_type=MESH)

    heads = nx * 16
    row = lax.broadcasted_iota(jnp.int32, (heads, 128), 0)
    lane = lax.broadcasted_iota(jnp.int32, (heads, 128), 1)
    q_heads = q_ref[...].astype(F32).reshape(heads, DH)
    m_heads = m_ref[...].astype(F32).reshape(heads, DH)
    o_heads = o_ref[...].astype(F32).reshape(heads, DH)
    delta = jnp.sum(m_heads * o_heads, axis=1, keepdims=True)
    lse_row = lse_ref[...].astype(F32) * LOG2E
    square_row = lax.broadcasted_iota(jnp.int32, (heads, heads), 0)
    square_lane = lax.broadcasted_iota(jnp.int32, (heads, heads), 1)
    lse_col = jnp.sum(
        jnp.where(square_row == square_lane, jnp.broadcast_to(lse_row, (heads, heads)), 0.0),
        axis=1, keepdims=True,
    )
    diagonal = lax.rem(lane, 8) == lax.rem(row, 8)

    def along_lanes(column):
        spread = jnp.where(diagonal, jnp.broadcast_to(column, (heads, 128)), 0.0)
        return jnp.sum(spread.reshape(heads // 8, 8, 128), axis=1)

    lse_lanes = along_lanes(lse_col)
    delta_lanes = along_lanes(delta)
    for i in range(nx):
        send_rows[i, 0:16, :] = q_heads[16 * i : 16 * i + 16].astype(BF16)
        send_rows[i, 16:32, :] = m_heads[16 * i : 16 * i + 16].astype(BF16)
        for g in range(2):
            send_stats[i, 2 * g : 2 * g + 1, :] = lse_lanes[2 * i + g : 2 * i + g + 1]
            send_stats[i, 2 * g + 1 : 2 * g + 2, :] = delta_lanes[2 * i + g : 2 * i + g + 1]

    pl.semaphore_wait(barrier, len(partners))

    mine = x * ny + y

    def xy_copies(i, dx, dy):
        x_to, y_to = xy_to(dx, dy)
        to = device(x_to, y_to, z, core)
        return (
            pltpu.make_async_remote_copy(
                src_ref=send_rows.at[x_to], dst_ref=recv_rows.at[mine],
                send_sem=xy_send.at[i], recv_sem=xy_recv.at[i],
                device_id=to, device_id_type=MESH,
            ),
            pltpu.make_async_remote_copy(
                src_ref=send_stats.at[x_to], dst_ref=recv_stats.at[mine],
                send_sem=xys_send.at[i], recv_sem=xys_recv.at[i],
                device_id=to, device_id_type=MESH,
            ),
        )

    pending = []
    for i, (dx, dy) in enumerate(xy_offsets):
        for copy in xy_copies(i, dx, dy):
            copy.start()
            pending.append(copy)
    sibling = device(x, y, z, other)

    def to_sibling(source, target, send, recv):
        return pltpu.make_async_remote_copy(
            src_ref=source, dst_ref=target, send_sem=send, recv_sem=recv,
            device_id=sibling, device_id_type=MESH,
        )

    shared = [
        to_sibling(source, target.at[1], kv_send.at[i], kv_recv.at[i])
        for i, (source, target) in enumerate(((k_hbm, k_ref), (v_hbm, v_ref)))
    ]
    for copy in shared:
        copy.start()
    recv_rows[mine] = send_rows[x]
    recv_stats[mine] = send_stats[x]
    q_all[...] = jnp.zeros_like(q_all)
    m_all[...] = jnp.zeros_like(m_all)
    for copy in pending:
        copy.wait_recv()

    stride = nz * CORES
    place = z * CORES + core
    starts, counts = [], []
    total = jnp.int32(0)
    for h in range(nx):
        live = lax.div(len_ref[h] - place + (stride - 1), stride)
        live = jnp.minimum(jnp.maximum(live, 0), ny)
        starts.append(total)
        counts.append(live)
        total = total + live

    stat_lane = lax.broadcasted_iota(jnp.int32, (4, 128), 1)

    def slot_rows(s):
        sample = jnp.int32(0)
        first = jnp.int32(0)
        for h in range(1, nx):
            past = s >= starts[h]
            sample = jnp.where(past, h, sample)
            first = jnp.where(past, starts[h], first)
        valid = s < total
        index = jnp.where(valid, sample * ny + (s - first), 0)
        packet = recv_rows[index].astype(F32).reshape(4, 8, 128)
        packet = jnp.where(valid, packet, 0.0)
        stat = jnp.where(jnp.logical_and(lax.div(stat_lane, 8) == s, valid), recv_stats[index], 0.0)
        return packet, stat

    stats = jnp.zeros((4, 128), F32)
    for s in range(0, slots, 2):
        first, stat = slot_rows(s)
        second, stat_second = slot_rows(s + 1)
        stats = stats + stat + stat_second
        for part in range(2):
            for g in range(2):
                both = jnp.concatenate([first[2 * part + g], second[2 * part + g]], axis=0)
                rows_all[z, part, g, 8 * s : 8 * s + 16, :] = both.astype(BF16)
    stats_all[z] = stats

    def when(condition, action):
        if isinstance(condition, bool):
            if condition:
                action()
        else:
            pl.when(condition)(action)

    def start(copies):
        for copy in copies:
            copy.start()

    def ring_copies(direction, hop, part, arriving=False):
        step = 1 if direction == 0 else -1
        block = at_z(-step * (hop if arriving else hop - 1))
        to = device(x, y, at_z(step), core)
        copies = [
            pltpu.make_async_remote_copy(
                src_ref=rows_all.at[block, part], dst_ref=rows_all.at[block, part],
                send_sem=ring_send.at[direction, hop, part],
                recv_sem=ring_recv.at[direction, hop, part],
                device_id=to, device_id_type=MESH,
            )
        ]
        if part == 0:
            copies.append(
                pltpu.make_async_remote_copy(
                    src_ref=stats_all.at[block], dst_ref=stats_all.at[block],
                    send_sem=rings_send.at[direction, hop], recv_sem=rings_recv.at[direction, hop],
                    device_id=to, device_id_type=MESH,
                )
            )
        return copies

    def advance(part, hop):
        for copy in ring_copies(0, hop, part, arriving=True):
            copy.wait_recv()
        when(hop < half, lambda: start(ring_copies(0, hop + 1, part)))

        def leftward():
            for copy in ring_copies(1, hop, part, arriving=True):
                copy.wait_recv()
            when(hop + 1 < half, lambda: start(ring_copies(1, hop + 1, part)))

        when(hop < half, leftward)

    block_width = 2 * unit
    middle_width = 2 * block_width
    own_at = (half - 1) * middle_width
    far_at = own_at + block_width
    columns = far_at + block_width
    far_from = far_at // 128 * 128

    def gather(offsets, at):
        for part, held in enumerate((q_all, m_all)):
            for n, offset in enumerate(offsets):
                for g in range(2):
                    to = at + n * block_width + g * unit
                    if not isinstance(to, int):
                        to = pl.multiple_of(to, 16)
                    held[pl.ds(to, unit), g * DH : (g + 1) * DH] = rows_all[at_z(offset), part, g]

    def stat_lanes(offsets):
        pieces = [
            stats_all[at_z(offset)][2 * g : 2 * g + 2, :unit]
            for offset in offsets for g in range(2)
        ]
        return jnp.concatenate(pieces, axis=1)

    def front(at, width, side):
        if isinstance(at, int):
            here = pl.ds(at, width)
        else:
            here = pl.ds(pl.multiple_of(at, 128), width)
        k = k_ref[side]
        scores = lax.dot_general(k, q_all[here, :], NT, preferred_element_type=F32)
        weights = jnp.exp2(scores * (scale * LOG2E) - stat_all[0:1, here])
        probs[side, :, here] = weights.astype(BF16)
        d_weights = lax.dot_general(v_ref[side], m_all[here, :], NT, preferred_element_type=F32)
        d_score = (weights * (d_weights - stat_all[1:2, here])).astype(BF16)
        d_scores[side, :, here] = d_score
        return lax.dot_general(d_score, k, TN, preferred_element_type=F32)

    def back(side, index):
        here = pl.ds(pl.multiple_of(index * tile, tile), tile)
        d_v = jnp.dot(probs[side, here, :], m_all[...], preferred_element_type=F32)
        d_k = jnp.dot(d_scores[side, here, :], q_all[...], preferred_element_type=F32)
        return here, d_v, d_k

    def z_copy(offset):
        return pltpu.make_async_remote_copy(
            src_ref=z_send.at[offset], dst_ref=z_recv.at[offset],
            send_sem=z_ssem.at[offset], recv_sem=z_rsem.at[offset],
            device_id=device(x, y, at_z(offset), core), device_id_type=MESH,
        )

    def give(offsets, d_query):
        for n, offset in enumerate(offsets):
            for g in range(2):
                low = n * block_width + g * unit
                z_send[offset, g] = d_query[low : low + unit, g * DH : (g + 1) * DH].astype(BF16)
            z_copy(offset).start()

    for part in range(2):
        start(ring_copies(0, 1, part))
        if half > 1:
            start(ring_copies(1, 1, part))
    gather([0], own_at)
    stat_all[:, own_at:far_at] = stat_lanes([0])
    load_k.wait()
    load_v.wait()
    d_query = front(own_at, block_width, 0)
    for g in range(2):
        dq_own[g] = d_query[g * unit : (g + 1) * unit, g * DH : (g + 1) * DH]
    for copy in shared:
        copy.wait_recv()
    d_query = front(own_at, block_width, 1)
    for g in range(2):
        dq_own[g] += d_query[g * unit : (g + 1) * unit, g * DH : (g + 1) * DH]
    advance(0, 1)

    def middle(hop, carry):
        offsets = [hop, nz - hop]
        at = (hop - 1) * middle_width
        advance(1, hop)
        gather(offsets, at)
        stat_all[:, pl.ds(pl.multiple_of(at, 128), middle_width)] = stat_lanes(offsets)
        dq_half[...] = front(at, middle_width, 0)
        advance(0, hop + 1)
        give(offsets, dq_half[...] + front(at, middle_width, 1))
        return carry

    lax.fori_loop(1, half, middle, 0)

    advance(1, half)
    gather([half], far_at)
    stat_all[:, own_at:columns] = stat_lanes([0, half])
    far_width = columns - far_from
    dq_half[0:far_width] = front(far_from, far_width, 0)
    d_query = dq_half[0:far_width] + front(far_from, far_width, 1)
    give([half], d_query[far_at - far_from :])

    tiles = ctx_len // tile

    def give_copies(index):
        here = pl.ds(pl.multiple_of(index * tile, tile), tile)
        return (
            to_sibling(dv_give.at[here], dv_got.at[here], give_send.at[0, index], give_recv.at[0, index]),
            to_sibling(dk_give.at[here], dk_got.at[here], give_send.at[1, index], give_recv.at[1, index]),
        )

    def stores(index):
        here = pl.ds(pl.multiple_of(index * tile, tile), tile)
        return (
            pltpu.make_async_copy(dv_out.at[here], dv_hbm.at[here], store_sem.at[0, index]),
            pltpu.make_async_copy(dk_out.at[here], dk_hbm.at[here], store_sem.at[1, index]),
        )

    def give_tile(index, carry):
        here, d_v, d_k = back(1, index)
        dv_give[here, :] = d_v.astype(BF16)
        dk_give[here, :] = d_k.astype(BF16)
        start(give_copies(index))
        return carry

    def own_tile(index, carry):
        here, d_v, d_k = back(0, index)
        for copy in give_copies(index):
            copy.wait_recv()
        dv_out[here, :] = (d_v + dv_got[here, :].astype(F32)).astype(BF16)
        dk_out[here, :] = ((d_k + dk_got[here, :].astype(F32)) * scale).astype(BF16)
        start(stores(index))
        return carry

    lax.fori_loop(0, tiles, give_tile, 0)
    lax.fori_loop(0, tiles // 2, own_tile, 0)

    result = dq_own[...]
    for offset in range(1, nz):
        z_copy(offset).wait_recv()
        result = result + z_recv[offset].astype(F32)
    for g in range(2):
        reduced[:, 8 * g : 8 * g + 8, :] = result[g].reshape(slots, 8, 128)

    for h in range(nx):
        for row_y in range(ny):
            valid = row_y < counts[h]
            slot = jnp.where(valid, starts[h] + row_y, 0)
            back_send[h * ny + row_y] = jnp.where(valid, reduced[slot], 0.0).astype(BF16)

    def back_copy(i, dx, dy):
        x_to, y_to = xy_to(dx, dy)
        return pltpu.make_async_remote_copy(
            src_ref=back_send.at[x_to * ny + y_to], dst_ref=back_recv.at[mine],
            send_sem=back_ssem.at[i], recv_sem=back_rsem.at[i],
            device_id=device(x_to, y_to, z, core), device_id_type=MESH,
        )

    backs = [back_copy(i, dx, dy) for i, (dx, dy) in enumerate(xy_offsets)]
    start(backs)
    back_recv[mine] = back_send[mine]
    lax.fori_loop(tiles // 2, tiles, own_tile, 0)
    for copy in backs:
        copy.wait_recv()
    for i in range(nx):
        owned = back_recv[i * ny].astype(F32)
        for row_y in range(1, ny):
            owned = owned + back_recv[i * ny + row_y].astype(F32)
        dq_ref[:, 16 * DH * i : 16 * DH * (i + 1)] = (owned * scale).reshape(1, 16 * DH).astype(BF16)

    for copy in pending + backs + shared:
        copy.wait_send()
    for part in range(2):
        for hop in range(1, half + 1):
            for copy in ring_copies(0, hop, part):
                copy.wait_send()
            if hop < half:
                for copy in ring_copies(1, hop, part):
                    copy.wait_send()
    for offset in range(1, nz):
        z_copy(offset).wait_send()

    def stored(index, carry):
        for copy in stores(index):
            copy.wait()
        for copy in give_copies(index):
            copy.wait_send()
        return carry

    lax.fori_loop(0, tiles, stored, 0)


def fused(nx, ny, nz, slots, tile, lengths, q, m, o, lse, keys, values):
    ctx_len, kv_cols = keys.shape
    unit = slots * 8
    columns = 2 * nz * unit
    vmem = pl.BlockSpec(memory_space=pltpu.VMEM)
    smem = pl.BlockSpec(memory_space=pltpu.SMEM)
    hbm = pl.BlockSpec(memory_space=pl.ANY)
    dma = pltpu.SemaphoreType.DMA
    packets = nx * ny
    half = nz // 2
    tiles = ctx_len // tile
    scratch = [
        pltpu.VMEM((CORES, ctx_len, kv_cols), BF16),
        pltpu.VMEM((CORES, ctx_len, kv_cols), BF16),
    ] + [pltpu.VMEM((ctx_len, kv_cols), BF16)] * 6 + [
        pltpu.VMEM((nx, 32, 128), BF16),
        pltpu.VMEM((nx, 4, 128), F32),
        pltpu.VMEM((packets, 32, 128), BF16),
        pltpu.VMEM((packets, 4, 128), F32),
        pltpu.VMEM((nz, 2, 2, unit, 128), BF16),
        pltpu.VMEM((nz, 4, 128), F32),
        pltpu.VMEM((columns, kv_cols), BF16),
        pltpu.VMEM((columns, kv_cols), BF16),
        pltpu.VMEM((2, columns), F32),
        pltpu.VMEM((CORES, ctx_len, columns), BF16),
        pltpu.VMEM((CORES, ctx_len, columns), BF16),
        pltpu.VMEM((4 * unit, kv_cols), F32),
        pltpu.VMEM((2, unit, 128), F32),
        pltpu.VMEM((nz, 2, unit, 128), BF16),
        pltpu.VMEM((nz, 2, unit, 128), BF16),
        pltpu.VMEM((slots, 16, 128), F32),
        pltpu.VMEM((packets, 16, 128), BF16),
        pltpu.VMEM((packets, 16, 128), BF16),
        dma((2,)), dma((2, tiles)), dma((2,)), dma((2,)), dma((2, tiles)), dma((2, tiles)),
        dma((packets,)), dma((packets,)), dma((packets,)), dma((packets,)),
        dma((2, half + 1, 2)), dma((2, half + 1, 2)), dma((2, half + 1)), dma((2, half + 1)),
        dma((nz,)), dma((nz,)),
        dma((packets,)), dma((packets,)),
    ]
    flops = 5 * 2 * ctx_len * 128 * 2 * unit * 2 * nz
    return pl.pallas_call(
        functools.partial(kernel, nx, ny, nz, slots, tile),
        out_shape=(
            jax.ShapeDtypeStruct(q.shape, BF16),
            jax.ShapeDtypeStruct(keys.shape, BF16),
            jax.ShapeDtypeStruct(values.shape, BF16),
        ),
        in_specs=[smem, vmem, vmem, vmem, vmem, hbm, hbm],
        out_specs=(vmem, hbm, hbm),
        scratch_shapes=scratch,
        compiler_params=pltpu.CompilerParams(
            collective_id=0, has_side_effects=True, vmem_limit_bytes=56 << 20
        ),
        cost_estimate=pl.CostEstimate(
            flops=flops, bytes_accessed=8 * ctx_len * kv_cols, transcendentals=0
        ),
    )(lengths, q, m, o, lse, keys, values)


def hand_over_kernel(dq_in, dk_in, dv_in, dq_out, dk_out, dv_out, dk_held, dv_held, sems):
    pieces = sems.shape[2]
    size = dk_in.shape[0] // pieces
    moves = []
    for i in range(pieces):
        here = pl.ds(i * size, size)
        for n, (source, held, target) in enumerate(
            ((dk_in, dk_held, dk_out), (dv_in, dv_held, dv_out))
        ):
            moves.append((
                pltpu.make_async_copy(source.at[here], held.at[here], sems.at[0, n, i]),
                pltpu.make_async_copy(held.at[here], target.at[here], sems.at[1, n, i]),
            ))
    for load, _ in moves:
        load.start()
    dq_out[...] = dq_in[...]
    for load, store in moves:
        load.wait()
        store.start()
    for _, store in moves:
        store.wait()


def hand_over(d_q, d_k, d_v, pieces=PIECES):
    vmem = pl.BlockSpec(memory_space=pltpu.VMEM)
    hbm = pl.BlockSpec(memory_space=pl.ANY)
    return pl.pallas_call(
        hand_over_kernel,
        out_shape=tuple(jax.ShapeDtypeStruct(a.shape, a.dtype) for a in (d_q, d_k, d_v)),
        in_specs=[vmem, hbm, hbm],
        out_specs=(vmem, hbm, hbm),
        scratch_shapes=[
            pltpu.VMEM(d_k.shape, BF16), pltpu.VMEM(d_v.shape, BF16),
            pltpu.SemaphoreType.DMA((2, 2, pieces)),
        ],
        compiler_params=pltpu.CompilerParams(vmem_limit_bytes=56 << 20),
    )(d_q, d_k, d_v)


def solution(mesh, nz=RING, slots=SLOTS, tile=TILE):
    nx = mesh.shape["head"]
    ny = mesh.shape["ctx"] // (nz * CORES)

    def on_device(queries, d_out, out_rows, lse, lengths, keys, values):
        d_q, d_k, d_v = fused(
            nx, ny, nz, slots, tile, lengths,
            queries, d_out, out_rows, lse, keys, values,
        )
        return hand_over(d_q, d_k, d_v)

    rows = P(("head", "ctx"), None)
    return jax.shard_map(
        on_device,
        mesh=mesh,
        in_specs=(rows, rows, rows, rows, P(), P("ctx", "head"), P("ctx", "head")),
        out_specs=(rows, P("ctx", "head"), P("ctx", "head")),
        check_vma=False,
    )
```

```python
import functools
import math

import jax
import jax.numpy as jnp
from jax import lax
from jax.experimental import pallas as pl
from jax.experimental.pallas import tpu as pltpu
from jax.sharding import PartitionSpec as P

DH = 128
CORES = 2
RING = 8
SLOTS = 12
TILE = 512
LOG2E = math.log2(math.e)
MESH = pl.DeviceIdType.MESH
F32 = jnp.float32
BF16 = jnp.bfloat16
NT = (((1,), (1,)), ((), ()))
TN = (((0,), (0,)), ((), ()))


def kernel(
    nx, ny, nz, slots, tile,
    len_ref, q_ref, m_ref, o_ref, lse_ref, k_hbm, v_hbm,
    dq_ref, dk_out, dv_out,
    k_ref, v_ref, dk_give, dv_give, dk_got, dv_got,
    send_rows, send_stats, recv_rows, recv_stats,
    rows_all, stats_all,
    q_all, m_all, stat_all, probs, d_scores, dq_half, dq_own,
    z_send, z_recv, reduced, back_send, back_recv,
    load_sem, kv_send, kv_recv, give_send, give_recv,
    xy_send, xy_recv, xys_send, xys_recv,
    ring_send, ring_recv, rings_send, rings_recv,
    z_ssem, z_rsem, back_ssem, back_rsem,
):
    x = lax.axis_index("head")
    c = lax.axis_index("ctx")
    core = lax.rem(c, CORES)
    z = lax.rem(lax.div(c, CORES), nz)
    y = lax.div(c, CORES * nz)
    other = 1 - core
    half = nz // 2
    ctx_len = k_ref.shape[1]
    unit = slots * 8
    scale = 1.0 / DH**0.5

    def device(x_to, y_to, z_to, core_to):
        return (x_to, (y_to * nz + z_to) * CORES + core_to)

    def at_z(offset):
        return lax.rem(z + offset + 2 * nz, nz)

    xy_offsets = [(dx, dy) for dx in range(nx) for dy in range(ny) if (dx, dy) != (0, 0)]

    def xy_to(dx, dy):
        return lax.rem(x + dx, nx), lax.rem(y + dy, ny)

    def xy_from(dx, dy):
        return lax.rem(x - dx + nx, nx), lax.rem(y - dy + ny, ny)

    load_k = pltpu.make_async_copy(k_hbm, k_ref.at[0], load_sem.at[0])
    load_v = pltpu.make_async_copy(v_hbm, v_ref.at[0], load_sem.at[1])
    load_k.start()
    load_v.start()

    barrier = pltpu.get_barrier_semaphore()
    partners = [device(*xy_to(dx, dy), z, core) for dx, dy in xy_offsets]
    partners += [device(x, y, at_z(dz), core) for dz in sorted({1, nz - 1})]
    partners += [device(x, y, z, other)]
    for partner in partners:
        pl.semaphore_signal(barrier, inc=1, device_id=partner, device_id_type=MESH)

    heads = nx * 16
    row = lax.broadcasted_iota(jnp.int32, (heads, 128), 0)
    lane = lax.broadcasted_iota(jnp.int32, (heads, 128), 1)
    q_heads = q_ref[...].astype(F32).reshape(heads, DH)
    m_heads = m_ref[...].astype(F32).reshape(heads, DH)
    o_heads = o_ref[...].astype(F32).reshape(heads, DH)
    delta = jnp.sum(m_heads * o_heads, axis=1, keepdims=True)
    lse_row = lse_ref[...].astype(F32) * LOG2E
    square_row = lax.broadcasted_iota(jnp.int32, (heads, heads), 0)
    square_lane = lax.broadcasted_iota(jnp.int32, (heads, heads), 1)
    lse_col = jnp.sum(
        jnp.where(square_row == square_lane, jnp.broadcast_to(lse_row, (heads, heads)), 0.0),
        axis=1, keepdims=True,
    )
    diagonal = lax.rem(lane, 8) == lax.rem(row, 8)

    def along_lanes(column):
        spread = jnp.where(diagonal, jnp.broadcast_to(column, (heads, 128)), 0.0)
        return jnp.sum(spread.reshape(heads // 8, 8, 128), axis=1)

    lse_lanes = along_lanes(lse_col)
    delta_lanes = along_lanes(delta)
    for i in range(nx):
        send_rows[i, 0:16, :] = q_heads[16 * i : 16 * i + 16].astype(BF16)
        send_rows[i, 16:32, :] = m_heads[16 * i : 16 * i + 16].astype(BF16)
        for g in range(2):
            send_stats[i, 2 * g : 2 * g + 1, :] = lse_lanes[2 * i + g : 2 * i + g + 1]
            send_stats[i, 2 * g + 1 : 2 * g + 2, :] = delta_lanes[2 * i + g : 2 * i + g + 1]

    pl.semaphore_wait(barrier, len(partners))

    mine = x * ny + y

    def xy_copies(i, dx, dy):
        x_to, y_to = xy_to(dx, dy)
        to = device(x_to, y_to, z, core)
        return (
            pltpu.make_async_remote_copy(
                src_ref=send_rows.at[x_to], dst_ref=recv_rows.at[mine],
                send_sem=xy_send.at[i], recv_sem=xy_recv.at[i],
                device_id=to, device_id_type=MESH,
            ),
            pltpu.make_async_remote_copy(
                src_ref=send_stats.at[x_to], dst_ref=recv_stats.at[mine],
                send_sem=xys_send.at[i], recv_sem=xys_recv.at[i],
                device_id=to, device_id_type=MESH,
            ),
        )

    pending = []
    for i, (dx, dy) in enumerate(xy_offsets):
        for copy in xy_copies(i, dx, dy):
            copy.start()
            pending.append(copy)
    sibling = device(x, y, z, other)

    def to_sibling(source, target, send, recv):
        return pltpu.make_async_remote_copy(
            src_ref=source, dst_ref=target, send_sem=send, recv_sem=recv,
            device_id=sibling, device_id_type=MESH,
        )

    shared = [
        to_sibling(source, target.at[1], kv_send.at[i], kv_recv.at[i])
        for i, (source, target) in enumerate(((k_hbm, k_ref), (v_hbm, v_ref)))
    ]
    for copy in shared:
        copy.start()
    recv_rows[mine] = send_rows[x]
    recv_stats[mine] = send_stats[x]
    q_all[...] = jnp.zeros_like(q_all)
    m_all[...] = jnp.zeros_like(m_all)
    for copy in pending:
        copy.wait_recv()

    stride = nz * CORES
    place = z * CORES + core
    starts, counts = [], []
    total = jnp.int32(0)
    for h in range(nx):
        live = lax.div(len_ref[h] - place + (stride - 1), stride)
        live = jnp.minimum(jnp.maximum(live, 0), ny)
        starts.append(total)
        counts.append(live)
        total = total + live

    stat_lane = lax.broadcasted_iota(jnp.int32, (4, 128), 1)

    def slot_rows(s):
        sample = jnp.int32(0)
        first = jnp.int32(0)
        for h in range(1, nx):
            past = s >= starts[h]
            sample = jnp.where(past, h, sample)
            first = jnp.where(past, starts[h], first)
        valid = s < total
        index = jnp.where(valid, sample * ny + (s - first), 0)
        packet = recv_rows[index].astype(F32).reshape(4, 8, 128)
        packet = jnp.where(valid, packet, 0.0)
        stat = jnp.where(jnp.logical_and(lax.div(stat_lane, 8) == s, valid), recv_stats[index], 0.0)
        return packet, stat

    stats = jnp.zeros((4, 128), F32)
    for s in range(0, slots, 2):
        first, stat = slot_rows(s)
        second, stat_second = slot_rows(s + 1)
        stats = stats + stat + stat_second
        for part in range(2):
            for g in range(2):
                both = jnp.concatenate([first[2 * part + g], second[2 * part + g]], axis=0)
                rows_all[z, part, g, 8 * s : 8 * s + 16, :] = both.astype(BF16)
    stats_all[z] = stats

    def when(condition, action):
        if isinstance(condition, bool):
            if condition:
                action()
        else:
            pl.when(condition)(action)

    def start(copies):
        for copy in copies:
            copy.start()

    def ring_copies(direction, hop, part, arriving=False):
        step = 1 if direction == 0 else -1
        block = at_z(-step * (hop if arriving else hop - 1))
        to = device(x, y, at_z(step), core)
        copies = [
            pltpu.make_async_remote_copy(
                src_ref=rows_all.at[block, part], dst_ref=rows_all.at[block, part],
                send_sem=ring_send.at[direction, hop, part],
                recv_sem=ring_recv.at[direction, hop, part],
                device_id=to, device_id_type=MESH,
            )
        ]
        if part == 0:
            copies.append(
                pltpu.make_async_remote_copy(
                    src_ref=stats_all.at[block], dst_ref=stats_all.at[block],
                    send_sem=rings_send.at[direction, hop], recv_sem=rings_recv.at[direction, hop],
                    device_id=to, device_id_type=MESH,
                )
            )
        return copies

    def advance(part, hop):
        for copy in ring_copies(0, hop, part, arriving=True):
            copy.wait_recv()
        when(hop < half, lambda: start(ring_copies(0, hop + 1, part)))

        def leftward():
            for copy in ring_copies(1, hop, part, arriving=True):
                copy.wait_recv()
            when(hop + 1 < half, lambda: start(ring_copies(1, hop + 1, part)))

        when(hop < half, leftward)

    block_width = 2 * unit
    middle_width = 2 * block_width
    own_at = (half - 1) * middle_width
    far_at = own_at + block_width
    columns = far_at + block_width
    far_from = far_at // 128 * 128

    def gather(offsets, at):
        for part, held in enumerate((q_all, m_all)):
            for n, offset in enumerate(offsets):
                for g in range(2):
                    to = at + n * block_width + g * unit
                    if not isinstance(to, int):
                        to = pl.multiple_of(to, 16)
                    held[pl.ds(to, unit), g * DH : (g + 1) * DH] = rows_all[at_z(offset), part, g]

    def stat_lanes(offsets):
        pieces = [
            stats_all[at_z(offset)][2 * g : 2 * g + 2, :unit]
            for offset in offsets for g in range(2)
        ]
        return jnp.concatenate(pieces, axis=1)

    def front(at, width, side):
        if isinstance(at, int):
            here = pl.ds(at, width)
        else:
            here = pl.ds(pl.multiple_of(at, 128), width)
        k = k_ref[side]
        scores = lax.dot_general(k, q_all[here, :], NT, preferred_element_type=F32)
        weights = jnp.exp2(scores * (scale * LOG2E) - stat_all[0:1, here])
        probs[side, :, here] = weights.astype(BF16)
        d_weights = lax.dot_general(v_ref[side], m_all[here, :], NT, preferred_element_type=F32)
        d_score = (weights * (d_weights - stat_all[1:2, here])).astype(BF16)
        d_scores[side, :, here] = d_score
        return lax.dot_general(d_score, k, TN, preferred_element_type=F32)

    def back(side, index):
        here = pl.ds(pl.multiple_of(index * tile, tile), tile)
        d_v = jnp.dot(probs[side, here, :], m_all[...], preferred_element_type=F32)
        d_k = jnp.dot(d_scores[side, here, :], q_all[...], preferred_element_type=F32)
        return here, d_v, d_k

    def z_copy(offset):
        return pltpu.make_async_remote_copy(
            src_ref=z_send.at[offset], dst_ref=z_recv.at[offset],
            send_sem=z_ssem.at[offset], recv_sem=z_rsem.at[offset],
            device_id=device(x, y, at_z(offset), core), device_id_type=MESH,
        )

    def give(offsets, d_query):
        for n, offset in enumerate(offsets):
            for g in range(2):
                low = n * block_width + g * unit
                z_send[offset, g] = d_query[low : low + unit, g * DH : (g + 1) * DH].astype(BF16)
            z_copy(offset).start()

    for part in range(2):
        start(ring_copies(0, 1, part))
        if half > 1:
            start(ring_copies(1, 1, part))
    gather([0], own_at)
    stat_all[:, own_at:far_at] = stat_lanes([0])
    load_k.wait()
    load_v.wait()
    d_query = front(own_at, block_width, 0)
    for g in range(2):
        dq_own[g] = d_query[g * unit : (g + 1) * unit, g * DH : (g + 1) * DH]
    for copy in shared:
        copy.wait_recv()
    d_query = front(own_at, block_width, 1)
    for g in range(2):
        dq_own[g] += d_query[g * unit : (g + 1) * unit, g * DH : (g + 1) * DH]
    advance(0, 1)
    advance(1, 1)

    def middle(hop, carry):
        offsets = [hop, nz - hop]
        at = (hop - 1) * middle_width
        gather(offsets, at)
        stat_all[:, pl.ds(pl.multiple_of(at, 128), middle_width)] = stat_lanes(offsets)
        dq_half[...] = front(at, middle_width, 0)
        advance(0, hop + 1)
        dq_half[...] += front(at, middle_width, 1)
        advance(1, hop + 1)
        give(offsets, dq_half[...])
        return carry

    lax.fori_loop(1, half, middle, 0)

    gather([half], far_at)
    stat_all[:, own_at:columns] = stat_lanes([0, half])
    far_width = columns - far_from
    dq_half[0:far_width] = front(far_from, far_width, 0)
    d_query = dq_half[0:far_width] + front(far_from, far_width, 1)
    give([half], d_query[far_at - far_from :])

    tiles = ctx_len // tile

    def give_copies(index):
        here = pl.ds(pl.multiple_of(index * tile, tile), tile)
        return (
            to_sibling(dv_give.at[here], dv_got.at[here], give_send.at[0, index], give_recv.at[0, index]),
            to_sibling(dk_give.at[here], dk_got.at[here], give_send.at[1, index], give_recv.at[1, index]),
        )

    def give_tile(index, carry):
        here, d_v, d_k = back(1, index)
        dv_give[here, :] = d_v.astype(BF16)
        dk_give[here, :] = d_k.astype(BF16)
        start(give_copies(index))
        return carry

    def own_tile(index, carry):
        here, d_v, d_k = back(0, index)
        for copy in give_copies(index):
            copy.wait_recv()
        dv_out[here, :] = (d_v + dv_got[here, :].astype(F32)).astype(BF16)
        dk_out[here, :] = ((d_k + dk_got[here, :].astype(F32)) * scale).astype(BF16)
        return carry

    lax.fori_loop(0, tiles, give_tile, 0)
    lax.fori_loop(0, tiles // 4, own_tile, 0)

    result = dq_own[...]
    for offset in range(1, nz):
        z_copy(offset).wait_recv()
        result = result + z_recv[offset].astype(F32)
    for g in range(2):
        reduced[:, 8 * g : 8 * g + 8, :] = result[g].reshape(slots, 8, 128)

    for h in range(nx):
        for row_y in range(ny):
            valid = row_y < counts[h]
            slot = jnp.where(valid, starts[h] + row_y, 0)
            back_send[h * ny + row_y] = jnp.where(valid, reduced[slot], 0.0).astype(BF16)

    def back_copy(i, dx, dy):
        x_to, y_to = xy_to(dx, dy)
        return pltpu.make_async_remote_copy(
            src_ref=back_send.at[x_to * ny + y_to], dst_ref=back_recv.at[mine],
            send_sem=back_ssem.at[i], recv_sem=back_rsem.at[i],
            device_id=device(x_to, y_to, z, core), device_id_type=MESH,
        )

    backs = [back_copy(i, dx, dy) for i, (dx, dy) in enumerate(xy_offsets)]
    start(backs)
    back_recv[mine] = back_send[mine]
    lax.fori_loop(tiles // 4, tiles, own_tile, 0)
    for copy in backs:
        copy.wait_recv()
    for i in range(nx):
        owned = back_recv[i * ny].astype(F32)
        for row_y in range(1, ny):
            owned = owned + back_recv[i * ny + row_y].astype(F32)
        dq_ref[:, 16 * DH * i : 16 * DH * (i + 1)] = (owned * scale).reshape(1, 16 * DH).astype(BF16)

    for copy in pending + backs + shared:
        copy.wait_send()
    for part in range(2):
        for hop in range(1, half + 1):
            for copy in ring_copies(0, hop, part):
                copy.wait_send()
            if hop < half:
                for copy in ring_copies(1, hop, part):
                    copy.wait_send()
    for offset in range(1, nz):
        z_copy(offset).wait_send()

    def gave(index, carry):
        for copy in give_copies(index):
            copy.wait_send()
        return carry

    lax.fori_loop(0, tiles, gave, 0)


def fused(nx, ny, nz, slots, tile, lengths, q, m, o, lse, keys, values):
    ctx_len, kv_cols = keys.shape
    unit = slots * 8
    columns = 2 * nz * unit
    vmem = pl.BlockSpec(memory_space=pltpu.VMEM)
    smem = pl.BlockSpec(memory_space=pltpu.SMEM)
    hbm = pl.BlockSpec(memory_space=pl.ANY)
    dma = pltpu.SemaphoreType.DMA
    packets = nx * ny
    half = nz // 2
    tiles = ctx_len // tile
    scratch = [
        pltpu.VMEM((CORES, ctx_len, kv_cols), BF16),
        pltpu.VMEM((CORES, ctx_len, kv_cols), BF16),
    ] + [pltpu.VMEM((ctx_len, kv_cols), BF16)] * 4 + [
        pltpu.VMEM((nx, 32, 128), BF16),
        pltpu.VMEM((nx, 4, 128), F32),
        pltpu.VMEM((packets, 32, 128), BF16),
        pltpu.VMEM((packets, 4, 128), F32),
        pltpu.VMEM((nz, 2, 2, unit, 128), BF16),
        pltpu.VMEM((nz, 4, 128), F32),
        pltpu.VMEM((columns, kv_cols), BF16),
        pltpu.VMEM((columns, kv_cols), BF16),
        pltpu.VMEM((2, columns), F32),
        pltpu.VMEM((CORES, ctx_len, columns), BF16),
        pltpu.VMEM((CORES, ctx_len, columns), BF16),
        pltpu.VMEM((4 * unit, kv_cols), F32),
        pltpu.VMEM((2, unit, 128), F32),
        pltpu.VMEM((nz, 2, unit, 128), BF16),
        pltpu.VMEM((nz, 2, unit, 128), BF16),
        pltpu.VMEM((slots, 16, 128), F32),
        pltpu.VMEM((packets, 16, 128), BF16),
        pltpu.VMEM((packets, 16, 128), BF16),
        dma((2,)), dma((2,)), dma((2,)), dma((2, tiles)), dma((2, tiles)),
        dma((packets,)), dma((packets,)), dma((packets,)), dma((packets,)),
        dma((2, half + 1, 2)), dma((2, half + 1, 2)), dma((2, half + 1)), dma((2, half + 1)),
        dma((nz,)), dma((nz,)),
        dma((packets,)), dma((packets,)),
    ]
    flops = 5 * 2 * ctx_len * 128 * 2 * unit * 2 * nz
    return pl.pallas_call(
        functools.partial(kernel, nx, ny, nz, slots, tile),
        out_shape=(
            jax.ShapeDtypeStruct(q.shape, BF16),
            pltpu.VMEM(keys.shape, BF16),
            pltpu.VMEM(values.shape, BF16),
        ),
        in_specs=[smem, vmem, vmem, vmem, vmem, hbm, hbm],
        out_specs=(vmem, vmem, vmem),
        scratch_shapes=scratch,
        compiler_params=pltpu.CompilerParams(
            collective_id=0, has_side_effects=True, vmem_limit_bytes=56 << 20
        ),
        cost_estimate=pl.CostEstimate(
            flops=flops, bytes_accessed=8 * ctx_len * kv_cols, transcendentals=0
        ),
    )(lengths, q, m, o, lse, keys, values)


def hand_over_kernel(dq_in, dk_in, dv_in, dq_out, dk_out, dv_out, sems):
    copies = [
        pltpu.make_async_copy(dk_in, dk_out, sems.at[0]),
        pltpu.make_async_copy(dv_in, dv_out, sems.at[1]),
    ]
    for copy in copies:
        copy.start()
    dq_out[...] = dq_in[...]
    for copy in copies:
        copy.wait()


def hand_over(d_q, d_k, d_v):
    vmem = pl.BlockSpec(memory_space=pltpu.VMEM)
    hbm = pl.BlockSpec(memory_space=pl.ANY)
    return pl.pallas_call(
        hand_over_kernel,
        out_shape=tuple(
            pltpu.HBM(a.shape, a.dtype) if i else jax.ShapeDtypeStruct(a.shape, a.dtype)
            for i, a in enumerate((d_q, d_k, d_v))
        ),
        in_specs=[vmem, vmem, vmem],
        out_specs=(vmem, hbm, hbm),
        scratch_shapes=[pltpu.SemaphoreType.DMA((2,))],
        compiler_params=pltpu.CompilerParams(vmem_limit_bytes=8 << 20),
    )(d_q, d_k, d_v)


def solution(mesh, nz=RING, slots=SLOTS, tile=TILE):
    nx = mesh.shape["head"]
    ny = mesh.shape["ctx"] // (nz * CORES)

    def on_device(queries, d_out, out_rows, lse, lengths, keys, values):
        d_q, d_k, d_v = fused(
            nx, ny, nz, slots, tile, lengths,
            queries, d_out, out_rows, lse, keys, values,
        )
        return hand_over(d_q, d_k, d_v)

    rows = P(("head", "ctx"), None)
    return jax.shard_map(
        on_device,
        mesh=mesh,
        in_specs=(rows, rows, rows, rows, P(), P("ctx", "head"), P("ctx", "head")),
        out_specs=(rows, P("ctx", "head"), P("ctx", "head")),
        check_vma=False,
    )
```

```python
import functools
import math

import jax
import jax.numpy as jnp
from jax import lax
from jax.experimental import pallas as pl
from jax.experimental.pallas import tpu as pltpu
from jax.sharding import PartitionSpec as P

DH = 128
CORES = 2
RING = 8
SLOTS = 12
TILE = 512
LOG2E = math.log2(math.e)
MESH = pl.DeviceIdType.MESH
F32 = jnp.float32
BF16 = jnp.bfloat16
NT = (((1,), (1,)), ((), ()))
TN = (((0,), (0,)), ((), ()))


def kernel(
    nx, ny, nz, slots, tile,
    len_ref, q_ref, m_ref, o_ref, lse_ref, k_hbm, v_hbm,
    dq_ref, dk_out, dv_out,
    k_ref, v_ref, dk_give, dv_give, dk_got, dv_got,
    send_rows, send_stats, recv_rows, recv_stats,
    rows_all, stats_all,
    q_all, m_all, stat_all, probs, d_scores, dq_half, dq_own,
    z_send, z_recv, reduced, back_send, back_recv,
    load_sem, kv_send, kv_recv, give_send, give_recv,
    xy_send, xy_recv, xys_send, xys_recv,
    ring_send, ring_recv, rings_send, rings_recv,
    z_ssem, z_rsem, back_ssem, back_rsem,
):
    x = lax.axis_index("head")
    c = lax.axis_index("ctx")
    core = lax.rem(c, CORES)
    z = lax.rem(lax.div(c, CORES), nz)
    y = lax.div(c, CORES * nz)
    other = 1 - core
    half = nz // 2
    ctx_len = k_ref.shape[1]
    unit = slots * 8
    scale = 1.0 / DH**0.5

    def device(x_to, y_to, z_to, core_to):
        return (x_to, (y_to * nz + z_to) * CORES + core_to)

    def at_z(offset):
        return lax.rem(z + offset + 2 * nz, nz)

    xy_offsets = [(dx, dy) for dx in range(nx) for dy in range(ny) if (dx, dy) != (0, 0)]

    def xy_to(dx, dy):
        return lax.rem(x + dx, nx), lax.rem(y + dy, ny)

    def xy_from(dx, dy):
        return lax.rem(x - dx + nx, nx), lax.rem(y - dy + ny, ny)

    load_k = pltpu.make_async_copy(k_hbm, k_ref.at[0], load_sem.at[0])
    load_v = pltpu.make_async_copy(v_hbm, v_ref.at[0], load_sem.at[1])
    load_k.start()
    load_v.start()

    barrier = pltpu.get_barrier_semaphore()
    partners = [device(*xy_to(dx, dy), z, core) for dx, dy in xy_offsets]
    partners += [device(x, y, at_z(dz), core) for dz in sorted({1, nz - 1})]
    partners += [device(x, y, z, other)]
    for partner in partners:
        pl.semaphore_signal(barrier, inc=1, device_id=partner, device_id_type=MESH)

    heads = nx * 16
    row = lax.broadcasted_iota(jnp.int32, (heads, 128), 0)
    lane = lax.broadcasted_iota(jnp.int32, (heads, 128), 1)
    q_heads = q_ref[...].astype(F32).reshape(heads, DH)
    m_heads = m_ref[...].astype(F32).reshape(heads, DH)
    o_heads = o_ref[...].astype(F32).reshape(heads, DH)
    delta = jnp.sum(m_heads * o_heads, axis=1, keepdims=True)
    lse_row = lse_ref[...].astype(F32) * LOG2E
    square_row = lax.broadcasted_iota(jnp.int32, (heads, heads), 0)
    square_lane = lax.broadcasted_iota(jnp.int32, (heads, heads), 1)
    lse_col = jnp.sum(
        jnp.where(square_row == square_lane, jnp.broadcast_to(lse_row, (heads, heads)), 0.0),
        axis=1, keepdims=True,
    )
    diagonal = lax.rem(lane, 8) == lax.rem(row, 8)

    def along_lanes(column):
        spread = jnp.where(diagonal, jnp.broadcast_to(column, (heads, 128)), 0.0)
        return jnp.sum(spread.reshape(heads // 8, 8, 128), axis=1)

    lse_lanes = along_lanes(lse_col)
    delta_lanes = along_lanes(delta)
    for i in range(nx):
        send_rows[i, 0:16, :] = q_heads[16 * i : 16 * i + 16].astype(BF16)
        send_rows[i, 16:32, :] = m_heads[16 * i : 16 * i + 16].astype(BF16)
        for g in range(2):
            send_stats[i, 2 * g : 2 * g + 1, :] = lse_lanes[2 * i + g : 2 * i + g + 1]
            send_stats[i, 2 * g + 1 : 2 * g + 2, :] = delta_lanes[2 * i + g : 2 * i + g + 1]

    pl.semaphore_wait(barrier, len(partners))

    mine = x * ny + y

    def xy_copies(i, dx, dy):
        x_to, y_to = xy_to(dx, dy)
        to = device(x_to, y_to, z, core)
        return (
            pltpu.make_async_remote_copy(
                src_ref=send_rows.at[x_to], dst_ref=recv_rows.at[mine],
                send_sem=xy_send.at[i], recv_sem=xy_recv.at[i],
                device_id=to, device_id_type=MESH,
            ),
            pltpu.make_async_remote_copy(
                src_ref=send_stats.at[x_to], dst_ref=recv_stats.at[mine],
                send_sem=xys_send.at[i], recv_sem=xys_recv.at[i],
                device_id=to, device_id_type=MESH,
            ),
        )

    pending = []
    for i, (dx, dy) in enumerate(xy_offsets):
        for copy in xy_copies(i, dx, dy):
            copy.start()
            pending.append(copy)
    sibling = device(x, y, z, other)

    def to_sibling(source, target, send, recv):
        return pltpu.make_async_remote_copy(
            src_ref=source, dst_ref=target, send_sem=send, recv_sem=recv,
            device_id=sibling, device_id_type=MESH,
        )

    shared = [
        to_sibling(source, target.at[1], kv_send.at[i], kv_recv.at[i])
        for i, (source, target) in enumerate(((k_hbm, k_ref), (v_hbm, v_ref)))
    ]
    for copy in shared:
        copy.start()
    recv_rows[mine] = send_rows[x]
    recv_stats[mine] = send_stats[x]
    q_all[...] = jnp.zeros_like(q_all)
    m_all[...] = jnp.zeros_like(m_all)
    for copy in pending:
        copy.wait_recv()

    stride = nz * CORES
    place = z * CORES + core
    starts, counts = [], []
    total = jnp.int32(0)
    for h in range(nx):
        live = lax.div(len_ref[h] - place + (stride - 1), stride)
        live = jnp.minimum(jnp.maximum(live, 0), ny)
        starts.append(total)
        counts.append(live)
        total = total + live

    stat_lane = lax.broadcasted_iota(jnp.int32, (4, 128), 1)

    picks = []
    for s in range(slots):
        sample = jnp.int32(0)
        first = jnp.int32(0)
        for h in range(1, nx):
            past = s >= starts[h]
            sample = jnp.where(past, h, sample)
            first = jnp.where(past, starts[h], first)
        valid = s < total
        picks.append((valid, jnp.where(valid, sample * ny + (s - first), 0)))

    def fill_stats():
        stats = jnp.zeros((4, 128), F32)
        for s, (valid, index) in enumerate(picks):
            ours = jnp.logical_and(lax.div(stat_lane, 8) == s, valid)
            stats = stats + jnp.where(ours, recv_stats[index], 0.0)
        stats_all[z] = stats

    def fill_rows(part):
        for s in range(0, slots, 2):
            pair = []
            for valid, index in picks[s : s + 2]:
                packet = recv_rows[index, 16 * part : 16 * part + 16, :].astype(F32)
                pair.append(jnp.where(valid, packet, 0.0))
            for g in range(2):
                both = jnp.concatenate([rows[8 * g : 8 * g + 8] for rows in pair], axis=0)
                rows_all[z, part, g, 8 * s : 8 * s + 16, :] = both.astype(BF16)

    def when(condition, action):
        if isinstance(condition, bool):
            if condition:
                action()
        else:
            pl.when(condition)(action)

    def start(copies):
        for copy in copies:
            copy.start()

    def ring_copies(direction, hop, part, arriving=False):
        step = 1 if direction == 0 else -1
        block = at_z(-step * (hop if arriving else hop - 1))
        to = device(x, y, at_z(step), core)
        copies = [
            pltpu.make_async_remote_copy(
                src_ref=rows_all.at[block, part], dst_ref=rows_all.at[block, part],
                send_sem=ring_send.at[direction, hop, part],
                recv_sem=ring_recv.at[direction, hop, part],
                device_id=to, device_id_type=MESH,
            )
        ]
        if part == 0:
            copies.append(
                pltpu.make_async_remote_copy(
                    src_ref=stats_all.at[block], dst_ref=stats_all.at[block],
                    send_sem=rings_send.at[direction, hop], recv_sem=rings_recv.at[direction, hop],
                    device_id=to, device_id_type=MESH,
                )
            )
        return copies

    def advance(part, hop):
        for copy in ring_copies(0, hop, part, arriving=True):
            copy.wait_recv()
        when(hop < half, lambda: start(ring_copies(0, hop + 1, part)))

        def leftward():
            for copy in ring_copies(1, hop, part, arriving=True):
                copy.wait_recv()
            when(hop + 1 < half, lambda: start(ring_copies(1, hop + 1, part)))

        when(hop < half, leftward)

    block_width = 2 * unit
    middle_width = 2 * block_width
    own_at = (half - 1) * middle_width
    far_at = own_at + block_width
    columns = far_at + block_width
    far_from = far_at // 128 * 128

    def gather(offsets, at):
        for part, held in enumerate((q_all, m_all)):
            for n, offset in enumerate(offsets):
                for g in range(2):
                    to = at + n * block_width + g * unit
                    if not isinstance(to, int):
                        to = pl.multiple_of(to, 16)
                    held[pl.ds(to, unit), g * DH : (g + 1) * DH] = rows_all[at_z(offset), part, g]

    def stat_lanes(offsets):
        pieces = [
            stats_all[at_z(offset)][2 * g : 2 * g + 2, :unit]
            for offset in offsets for g in range(2)
        ]
        return jnp.concatenate(pieces, axis=1)

    def front(at, width, side):
        if isinstance(at, int):
            here = pl.ds(at, width)
        else:
            here = pl.ds(pl.multiple_of(at, 128), width)
        k = k_ref[side]
        scores = lax.dot_general(k, q_all[here, :], NT, preferred_element_type=F32)
        weights = jnp.exp2(scores * (scale * LOG2E) - stat_all[0:1, here])
        probs[side, :, here] = weights.astype(BF16)
        d_weights = lax.dot_general(v_ref[side], m_all[here, :], NT, preferred_element_type=F32)
        d_score = (weights * (d_weights - stat_all[1:2, here])).astype(BF16)
        d_scores[side, :, here] = d_score
        return lax.dot_general(d_score, k, TN, preferred_element_type=F32)

    def back(side, index):
        here = pl.ds(pl.multiple_of(index * tile, tile), tile)
        d_v = jnp.dot(probs[side, here, :], m_all[...], preferred_element_type=F32)
        d_k = jnp.dot(d_scores[side, here, :], q_all[...], preferred_element_type=F32)
        return here, d_v, d_k

    def z_copy(offset):
        return pltpu.make_async_remote_copy(
            src_ref=z_send.at[offset], dst_ref=z_recv.at[offset],
            send_sem=z_ssem.at[offset], recv_sem=z_rsem.at[offset],
            device_id=device(x, y, at_z(offset), core), device_id_type=MESH,
        )

    def give(offsets, d_query):
        for n, offset in enumerate(offsets):
            for g in range(2):
                low = n * block_width + g * unit
                z_send[offset, g] = d_query[low : low + unit, g * DH : (g + 1) * DH].astype(BF16)
            z_copy(offset).start()

    for part in range(2):
        if part == 0:
            fill_stats()
        fill_rows(part)
        start(ring_copies(0, 1, part))
        if half > 1:
            start(ring_copies(1, 1, part))
    gather([0], own_at)
    stat_all[:, own_at:far_at] = stat_lanes([0])
    load_k.wait()
    load_v.wait()
    d_query = front(own_at, block_width, 0)
    for g in range(2):
        dq_own[g] = d_query[g * unit : (g + 1) * unit, g * DH : (g + 1) * DH]
    for copy in shared:
        copy.wait_recv()
    d_query = front(own_at, block_width, 1)
    for g in range(2):
        dq_own[g] += d_query[g * unit : (g + 1) * unit, g * DH : (g + 1) * DH]
    advance(0, 1)
    advance(1, 1)

    def middle(hop, carry):
        offsets = [hop, nz - hop]
        at = (hop - 1) * middle_width
        gather(offsets, at)
        stat_all[:, pl.ds(pl.multiple_of(at, 128), middle_width)] = stat_lanes(offsets)
        dq_half[...] = front(at, middle_width, 0)
        advance(0, hop + 1)
        dq_half[...] += front(at, middle_width, 1)
        advance(1, hop + 1)
        give(offsets, dq_half[...])
        return carry

    lax.fori_loop(1, half, middle, 0)

    gather([half], far_at)
    stat_all[:, own_at:columns] = stat_lanes([0, half])
    far_width = columns - far_from
    dq_half[0:far_width] = front(far_from, far_width, 0)
    d_query = dq_half[0:far_width] + front(far_from, far_width, 1)
    give([half], d_query[far_at - far_from :])

    tiles = ctx_len // tile

    def give_copies(index):
        here = pl.ds(pl.multiple_of(index * tile, tile), tile)
        return (
            to_sibling(dv_give.at[here], dv_got.at[here], give_send.at[0, index], give_recv.at[0, index]),
            to_sibling(dk_give.at[here], dk_got.at[here], give_send.at[1, index], give_recv.at[1, index]),
        )

    def give_tile(index, carry):
        here, d_v, d_k = back(1, index)
        dv_give[here, :] = d_v.astype(BF16)
        dk_give[here, :] = d_k.astype(BF16)
        start(give_copies(index))
        return carry

    def own_tile(index, carry):
        here, d_v, d_k = back(0, index)
        for copy in give_copies(index):
            copy.wait_recv()
        dv_out[here, :] = (d_v + dv_got[here, :].astype(F32)).astype(BF16)
        dk_out[here, :] = ((d_k + dk_got[here, :].astype(F32)) * scale).astype(BF16)
        return carry

    lax.fori_loop(0, tiles, give_tile, 0)
    lax.fori_loop(0, tiles // 4, own_tile, 0)

    result = dq_own[...]
    for offset in range(1, nz):
        z_copy(offset).wait_recv()
        result = result + z_recv[offset].astype(F32)
    for g in range(2):
        reduced[:, 8 * g : 8 * g + 8, :] = result[g].reshape(slots, 8, 128)

    for h in range(nx):
        for row_y in range(ny):
            valid = row_y < counts[h]
            slot = jnp.where(valid, starts[h] + row_y, 0)
            back_send[h * ny + row_y] = jnp.where(valid, reduced[slot], 0.0).astype(BF16)

    def back_copy(i, dx, dy):
        x_to, y_to = xy_to(dx, dy)
        return pltpu.make_async_remote_copy(
            src_ref=back_send.at[x_to * ny + y_to], dst_ref=back_recv.at[mine],
            send_sem=back_ssem.at[i], recv_sem=back_rsem.at[i],
            device_id=device(x_to, y_to, z, core), device_id_type=MESH,
        )

    backs = [back_copy(i, dx, dy) for i, (dx, dy) in enumerate(xy_offsets)]
    start(backs)
    back_recv[mine] = back_send[mine]
    lax.fori_loop(tiles // 4, tiles, own_tile, 0)

    for copy in pending + shared:
        copy.wait_send()
    for part in range(2):
        for hop in range(1, half + 1):
            for copy in ring_copies(0, hop, part):
                copy.wait_send()
            if hop < half:
                for copy in ring_copies(1, hop, part):
                    copy.wait_send()
    for offset in range(1, nz):
        z_copy(offset).wait_send()

    def gave(index, carry):
        for copy in give_copies(index):
            copy.wait_send()
        return carry

    lax.fori_loop(0, tiles, gave, 0)

    for copy in backs:
        copy.wait_recv()
    for i in range(nx):
        owned = back_recv[i * ny].astype(F32)
        for row_y in range(1, ny):
            owned = owned + back_recv[i * ny + row_y].astype(F32)
        dq_ref[:, 16 * DH * i : 16 * DH * (i + 1)] = (owned * scale).reshape(1, 16 * DH).astype(BF16)
    for copy in backs:
        copy.wait_send()


def fused(nx, ny, nz, slots, tile, lengths, q, m, o, lse, keys, values):
    ctx_len, kv_cols = keys.shape
    unit = slots * 8
    columns = 2 * nz * unit
    vmem = pl.BlockSpec(memory_space=pltpu.VMEM)
    smem = pl.BlockSpec(memory_space=pltpu.SMEM)
    hbm = pl.BlockSpec(memory_space=pl.ANY)
    dma = pltpu.SemaphoreType.DMA
    packets = nx * ny
    half = nz // 2
    tiles = ctx_len // tile
    scratch = [
        pltpu.VMEM((CORES, ctx_len, kv_cols), BF16),
        pltpu.VMEM((CORES, ctx_len, kv_cols), BF16),
    ] + [pltpu.VMEM((ctx_len, kv_cols), BF16)] * 4 + [
        pltpu.VMEM((nx, 32, 128), BF16),
        pltpu.VMEM((nx, 4, 128), F32),
        pltpu.VMEM((packets, 32, 128), BF16),
        pltpu.VMEM((packets, 4, 128), F32),
        pltpu.VMEM((nz, 2, 2, unit, 128), BF16),
        pltpu.VMEM((nz, 4, 128), F32),
        pltpu.VMEM((columns, kv_cols), BF16),
        pltpu.VMEM((columns, kv_cols), BF16),
        pltpu.VMEM((2, columns), F32),
        pltpu.VMEM((CORES, ctx_len, columns), BF16),
        pltpu.VMEM((CORES, ctx_len, columns), BF16),
        pltpu.VMEM((4 * unit, kv_cols), F32),
        pltpu.VMEM((2, unit, 128), F32),
        pltpu.VMEM((nz, 2, unit, 128), BF16),
        pltpu.VMEM((nz, 2, unit, 128), BF16),
        pltpu.VMEM((slots, 16, 128), F32),
        pltpu.VMEM((packets, 16, 128), BF16),
        pltpu.VMEM((packets, 16, 128), BF16),
        dma((2,)), dma((2,)), dma((2,)), dma((2, tiles)), dma((2, tiles)),
        dma((packets,)), dma((packets,)), dma((packets,)), dma((packets,)),
        dma((2, half + 1, 2)), dma((2, half + 1, 2)), dma((2, half + 1)), dma((2, half + 1)),
        dma((nz,)), dma((nz,)),
        dma((packets,)), dma((packets,)),
    ]
    flops = 5 * 2 * ctx_len * 128 * 2 * unit * 2 * nz
    return pl.pallas_call(
        functools.partial(kernel, nx, ny, nz, slots, tile),
        out_shape=(
            pltpu.VMEM(q.shape, BF16),
            pltpu.VMEM(keys.shape, BF16),
            pltpu.VMEM(values.shape, BF16),
        ),
        in_specs=[smem, vmem, vmem, vmem, vmem, hbm, hbm],
        out_specs=(vmem, vmem, vmem),
        scratch_shapes=scratch,
        compiler_params=pltpu.CompilerParams(
            collective_id=0, has_side_effects=True, vmem_limit_bytes=56 << 20
        ),
        cost_estimate=pl.CostEstimate(
            flops=flops, bytes_accessed=8 * ctx_len * kv_cols, transcendentals=0
        ),
    )(lengths, q, m, o, lse, keys, values)


def hand_over_kernel(dq_in, dk_in, dv_in, dq_out, dk_out, dv_out, sems):
    copies = [
        pltpu.make_async_copy(dk_in, dk_out, sems.at[0]),
        pltpu.make_async_copy(dv_in, dv_out, sems.at[1]),
    ]
    for copy in copies:
        copy.start()
    dq_out[...] = dq_in[...]
    for copy in copies:
        copy.wait()


def hand_over(d_q, d_k, d_v):
    vmem = pl.BlockSpec(memory_space=pltpu.VMEM)
    hbm = pl.BlockSpec(memory_space=pl.ANY)
    return pl.pallas_call(
        hand_over_kernel,
        out_shape=tuple(
            pltpu.HBM(a.shape, a.dtype) if i else jax.ShapeDtypeStruct(a.shape, a.dtype)
            for i, a in enumerate((d_q, d_k, d_v))
        ),
        in_specs=[vmem, vmem, vmem],
        out_specs=(vmem, hbm, hbm),
        scratch_shapes=[pltpu.SemaphoreType.DMA((2,))],
        compiler_params=pltpu.CompilerParams(vmem_limit_bytes=8 << 20),
    )(d_q, d_k, d_v)


def solution(mesh, nz=RING, slots=SLOTS, tile=TILE):
    nx = mesh.shape["head"]
    ny = mesh.shape["ctx"] // (nz * CORES)

    def on_device(queries, d_out, out_rows, lse, lengths, keys, values):
        d_q, d_k, d_v = fused(
            nx, ny, nz, slots, tile, lengths,
            queries, d_out, out_rows, lse, keys, values,
        )
        return hand_over(d_q, d_k, d_v)

    rows = P(("head", "ctx"), None)
    return jax.shard_map(
        on_device,
        mesh=mesh,
        in_specs=(rows, rows, rows, rows, P(), P("ctx", "head"), P("ctx", "head")),
        out_specs=(rows, P("ctx", "head"), P("ctx", "head")),
        check_vma=False,
    )
```

```python
import functools
import math

import jax
import jax.numpy as jnp
from jax import lax
from jax.experimental import pallas as pl
from jax.experimental.pallas import tpu as pltpu
from jax.sharding import PartitionSpec as P

DH = 128
CORES = 2
RING = 8
SLOTS = 12
TILE = 512
LOG2E = math.log2(math.e)
MESH = pl.DeviceIdType.MESH
F32 = jnp.float32
BF16 = jnp.bfloat16
NT = (((1,), (1,)), ((), ()))
TN = (((0,), (0,)), ((), ()))


def kernel(
    nx, ny, nz, slots, tile,
    len_ref, q_ref, m_ref, o_ref, lse_ref, k_hbm, v_hbm,
    dq_ref, dk_out, dv_out,
    k_ref, v_ref, dk_give, dv_give, dk_got, dv_got,
    send_rows, send_stats, recv_rows, recv_stats,
    rows_all, stats_all,
    q_all, m_all, stat_all, probs, d_scores, dq_half, dq_own,
    z_send, z_recv, reduced, back_send, back_recv,
    load_sem, kv_send, kv_recv, give_send, give_recv,
    xy_send, xy_recv, xys_send, xys_recv,
    ring_send, ring_recv, rings_send, rings_recv,
    z_ssem, z_rsem, back_ssem, back_rsem,
):
    x = lax.axis_index("head")
    c = lax.axis_index("ctx")
    core = lax.rem(c, CORES)
    z = lax.rem(lax.div(c, CORES), nz)
    y = lax.div(c, CORES * nz)
    other = 1 - core
    half = nz // 2
    ctx_len = k_ref.shape[1]
    unit = slots * 8
    scale = 1.0 / DH**0.5

    def device(x_to, y_to, z_to, core_to):
        return (x_to, (y_to * nz + z_to) * CORES + core_to)

    def at_z(offset):
        return lax.rem(z + offset + 2 * nz, nz)

    def hops(offset):
        return min(offset[0], nx - offset[0]) + min(offset[1], ny - offset[1])

    xy_offsets = [(dx, dy) for dx in range(nx) for dy in range(ny) if (dx, dy) != (0, 0)]
    xy_offsets.sort(key=hops, reverse=True)

    def xy_to(dx, dy):
        return lax.rem(x + dx, nx), lax.rem(y + dy, ny)

    def xy_from(dx, dy):
        return lax.rem(x - dx + nx, nx), lax.rem(y - dy + ny, ny)

    load_k = pltpu.make_async_copy(k_hbm, k_ref.at[0], load_sem.at[0])
    load_v = pltpu.make_async_copy(v_hbm, v_ref.at[0], load_sem.at[1])
    load_k.start()
    load_v.start()

    barrier = pltpu.get_barrier_semaphore()
    partners = [device(*xy_to(dx, dy), z, core) for dx, dy in xy_offsets]
    partners += [device(x, y, at_z(dz), core) for dz in sorted({1, nz - 1})]
    partners += [device(x, y, z, other)]
    for partner in partners:
        pl.semaphore_signal(barrier, inc=1, device_id=partner, device_id_type=MESH)

    heads = nx * 16
    row = lax.broadcasted_iota(jnp.int32, (heads, 128), 0)
    lane = lax.broadcasted_iota(jnp.int32, (heads, 128), 1)
    q_heads = q_ref[...].astype(F32).reshape(heads, DH)
    m_heads = m_ref[...].astype(F32).reshape(heads, DH)
    o_heads = o_ref[...].astype(F32).reshape(heads, DH)
    delta = jnp.sum(m_heads * o_heads, axis=1, keepdims=True)
    lse_row = lse_ref[...].astype(F32) * LOG2E
    square_row = lax.broadcasted_iota(jnp.int32, (heads, heads), 0)
    square_lane = lax.broadcasted_iota(jnp.int32, (heads, heads), 1)
    lse_col = jnp.sum(
        jnp.where(square_row == square_lane, jnp.broadcast_to(lse_row, (heads, heads)), 0.0),
        axis=1, keepdims=True,
    )
    diagonal = lax.rem(lane, 8) == lax.rem(row, 8)

    def along_lanes(column):
        spread = jnp.where(diagonal, jnp.broadcast_to(column, (heads, 128)), 0.0)
        return jnp.sum(spread.reshape(heads // 8, 8, 128), axis=1)

    lse_lanes = along_lanes(lse_col)
    delta_lanes = along_lanes(delta)
    for i in range(nx):
        send_rows[i, 0:16, :] = q_heads[16 * i : 16 * i + 16].astype(BF16)
        send_rows[i, 16:32, :] = m_heads[16 * i : 16 * i + 16].astype(BF16)
        for g in range(2):
            send_stats[i, 2 * g : 2 * g + 1, :] = lse_lanes[2 * i + g : 2 * i + g + 1]
            send_stats[i, 2 * g + 1 : 2 * g + 2, :] = delta_lanes[2 * i + g : 2 * i + g + 1]

    pl.semaphore_wait(barrier, len(partners))

    mine = x * ny + y

    def xy_copies(i, dx, dy):
        x_to, y_to = xy_to(dx, dy)
        to = device(x_to, y_to, z, core)
        return (
            pltpu.make_async_remote_copy(
                src_ref=send_rows.at[x_to], dst_ref=recv_rows.at[mine],
                send_sem=xy_send.at[i], recv_sem=xy_recv.at[i],
                device_id=to, device_id_type=MESH,
            ),
            pltpu.make_async_remote_copy(
                src_ref=send_stats.at[x_to], dst_ref=recv_stats.at[mine],
                send_sem=xys_send.at[i], recv_sem=xys_recv.at[i],
                device_id=to, device_id_type=MESH,
            ),
        )

    pending = []
    for i, (dx, dy) in enumerate(xy_offsets):
        for copy in xy_copies(i, dx, dy):
            copy.start()
            pending.append(copy)
    sibling = device(x, y, z, other)

    def to_sibling(source, target, send, recv):
        return pltpu.make_async_remote_copy(
            src_ref=source, dst_ref=target, send_sem=send, recv_sem=recv,
            device_id=sibling, device_id_type=MESH,
        )

    shared = [
        to_sibling(source, target.at[1], kv_send.at[i], kv_recv.at[i])
        for i, (source, target) in enumerate(((k_hbm, k_ref), (v_hbm, v_ref)))
    ]
    for copy in shared:
        copy.start()
    recv_rows[mine] = send_rows[x]
    recv_stats[mine] = send_stats[x]
    q_all[...] = jnp.zeros_like(q_all)
    m_all[...] = jnp.zeros_like(m_all)
    for copy in pending:
        copy.wait_recv()

    stride = nz * CORES
    place = z * CORES + core
    starts, counts = [], []
    total = jnp.int32(0)
    for h in range(nx):
        live = lax.div(len_ref[h] - place + (stride - 1), stride)
        live = jnp.minimum(jnp.maximum(live, 0), ny)
        starts.append(total)
        counts.append(live)
        total = total + live

    stat_lane = lax.broadcasted_iota(jnp.int32, (4, 128), 1)

    picks = []
    for s in range(slots):
        sample = jnp.int32(0)
        first = jnp.int32(0)
        for h in range(1, nx):
            past = s >= starts[h]
            sample = jnp.where(past, h, sample)
            first = jnp.where(past, starts[h], first)
        valid = s < total
        picks.append((valid, jnp.where(valid, sample * ny + (s - first), 0)))

    def fill_stats():
        stats = jnp.zeros((4, 128), F32)
        for s, (valid, index) in enumerate(picks):
            ours = jnp.logical_and(lax.div(stat_lane, 8) == s, valid)
            stats = stats + jnp.where(ours, recv_stats[index], 0.0)
        stats_all[z] = stats

    def fill_rows(part):
        for s in range(0, slots, 2):
            pair = []
            for valid, index in picks[s : s + 2]:
                packet = recv_rows[index, 16 * part : 16 * part + 16, :].astype(F32)
                pair.append(jnp.where(valid, packet, 0.0))
            for g in range(2):
                both = jnp.concatenate([rows[8 * g : 8 * g + 8] for rows in pair], axis=0)
                rows_all[z, part, g, 8 * s : 8 * s + 16, :] = both.astype(BF16)

    def when(condition, action):
        if isinstance(condition, bool):
            if condition:
                action()
        else:
            pl.when(condition)(action)

    def start(copies):
        for copy in copies:
            copy.start()

    def ring_copies(direction, hop, part, arriving=False):
        step = 1 if direction == 0 else -1
        block = at_z(-step * (hop if arriving else hop - 1))
        to = device(x, y, at_z(step), core)
        copies = [
            pltpu.make_async_remote_copy(
                src_ref=rows_all.at[block, part], dst_ref=rows_all.at[block, part],
                send_sem=ring_send.at[direction, hop, part],
                recv_sem=ring_recv.at[direction, hop, part],
                device_id=to, device_id_type=MESH,
            )
        ]
        if part == 0:
            copies.append(
                pltpu.make_async_remote_copy(
                    src_ref=stats_all.at[block], dst_ref=stats_all.at[block],
                    send_sem=rings_send.at[direction, hop], recv_sem=rings_recv.at[direction, hop],
                    device_id=to, device_id_type=MESH,
                )
            )
        return copies

    def advance(part, hop):
        for copy in ring_copies(0, hop, part, arriving=True):
            copy.wait_recv()
        when(hop < half, lambda: start(ring_copies(0, hop + 1, part)))

        def leftward():
            for copy in ring_copies(1, hop, part, arriving=True):
                copy.wait_recv()
            when(hop + 1 < half, lambda: start(ring_copies(1, hop + 1, part)))

        when(hop < half, leftward)

    block_width = 2 * unit
    middle_width = 2 * block_width
    own_at = (half - 1) * middle_width
    far_at = own_at + block_width
    columns = far_at + block_width
    far_from = far_at // 128 * 128

    def gather(offsets, at):
        for part, held in enumerate((q_all, m_all)):
            for n, offset in enumerate(offsets):
                for g in range(2):
                    to = at + n * block_width + g * unit
                    if not isinstance(to, int):
                        to = pl.multiple_of(to, 16)
                    held[pl.ds(to, unit), g * DH : (g + 1) * DH] = rows_all[at_z(offset), part, g]

    def stat_lanes(offsets):
        pieces = [
            stats_all[at_z(offset)][2 * g : 2 * g + 2, :unit]
            for offset in offsets for g in range(2)
        ]
        return jnp.concatenate(pieces, axis=1)

    def front(at, width, side):
        if isinstance(at, int):
            here = pl.ds(at, width)
        else:
            here = pl.ds(pl.multiple_of(at, 128), width)
        k = k_ref[side]
        scores = lax.dot_general(k, q_all[here, :], NT, preferred_element_type=F32)
        weights = jnp.exp2(scores * (scale * LOG2E) - stat_all[0:1, here])
        probs[side, :, here] = weights.astype(BF16)
        d_weights = lax.dot_general(v_ref[side], m_all[here, :], NT, preferred_element_type=F32)
        d_score = (weights * (d_weights - stat_all[1:2, here])).astype(BF16)
        d_scores[side, :, here] = d_score
        return lax.dot_general(d_score, k, TN, preferred_element_type=F32)

    def back(side, index):
        here = pl.ds(pl.multiple_of(index * tile, tile), tile)
        d_v = jnp.dot(probs[side, here, :], m_all[...], preferred_element_type=F32)
        d_k = jnp.dot(d_scores[side, here, :], q_all[...], preferred_element_type=F32)
        return here, d_v, d_k

    def z_copy(offset):
        return pltpu.make_async_remote_copy(
            src_ref=z_send.at[offset], dst_ref=z_recv.at[offset],
            send_sem=z_ssem.at[offset], recv_sem=z_rsem.at[offset],
            device_id=device(x, y, at_z(offset), core), device_id_type=MESH,
        )

    def give(offsets, d_query):
        for n, offset in enumerate(offsets):
            for g in range(2):
                low = n * block_width + g * unit
                z_send[offset, g] = d_query[low : low + unit, g * DH : (g + 1) * DH].astype(BF16)
            z_copy(offset).start()

    for part in range(2):
        if part == 0:
            fill_stats()
        fill_rows(part)
        start(ring_copies(0, 1, part))
        if half > 1:
            start(ring_copies(1, 1, part))
    gather([0], own_at)
    stat_all[:, own_at:far_at] = stat_lanes([0])
    load_k.wait()
    load_v.wait()
    d_query = front(own_at, block_width, 0)
    for g in range(2):
        dq_own[g] = d_query[g * unit : (g + 1) * unit, g * DH : (g + 1) * DH]
    for copy in shared:
        copy.wait_recv()
    d_query = front(own_at, block_width, 1)
    for g in range(2):
        dq_own[g] += d_query[g * unit : (g + 1) * unit, g * DH : (g + 1) * DH]
    advance(0, 1)
    advance(1, 1)

    def middle(hop, carry):
        offsets = [hop, nz - hop]
        at = (hop - 1) * middle_width
        gather(offsets, at)
        stat_all[:, pl.ds(pl.multiple_of(at, 128), middle_width)] = stat_lanes(offsets)
        dq_half[...] = front(at, middle_width, 0)
        advance(0, hop + 1)
        dq_half[...] += front(at, middle_width, 1)
        advance(1, hop + 1)
        give(offsets, dq_half[...])
        return carry

    lax.fori_loop(1, half, middle, 0)

    gather([half], far_at)
    stat_all[:, own_at:columns] = stat_lanes([0, half])
    far_width = columns - far_from
    dq_half[0:far_width] = front(far_from, far_width, 0)
    d_query = dq_half[0:far_width] + front(far_from, far_width, 1)
    give([half], d_query[far_at - far_from :])

    tiles = ctx_len // tile

    def give_copies(index):
        here = pl.ds(pl.multiple_of(index * tile, tile), tile)
        return (
            to_sibling(dv_give.at[here], dv_got.at[here], give_send.at[0, index], give_recv.at[0, index]),
            to_sibling(dk_give.at[here], dk_got.at[here], give_send.at[1, index], give_recv.at[1, index]),
        )

    def give_tile(index, carry):
        here, d_v, d_k = back(1, index)
        dv_give[here, :] = d_v.astype(BF16)
        dk_give[here, :] = d_k.astype(BF16)
        start(give_copies(index))
        return carry

    def own_tile(index, carry):
        here, d_v, d_k = back(0, index)
        for copy in give_copies(index):
            copy.wait_recv()
        dv_out[here, :] = (d_v + dv_got[here, :].astype(F32)).astype(BF16)
        dk_out[here, :] = ((d_k + dk_got[here, :].astype(F32)) * scale).astype(BF16)
        return carry

    lax.fori_loop(0, tiles, give_tile, 0)
    lax.fori_loop(0, tiles // 4, own_tile, 0)

    result = dq_own[...]
    for offset in range(1, nz):
        z_copy(offset).wait_recv()
        result = result + z_recv[offset].astype(F32)
    for g in range(2):
        reduced[:, 8 * g : 8 * g + 8, :] = result[g].reshape(slots, 8, 128)

    for h in range(nx):
        for row_y in range(ny):
            valid = row_y < counts[h]
            slot = jnp.where(valid, starts[h] + row_y, 0)
            back_send[h * ny + row_y] = jnp.where(valid, reduced[slot], 0.0).astype(BF16)

    def back_copy(i, dx, dy):
        x_to, y_to = xy_to(dx, dy)
        return pltpu.make_async_remote_copy(
            src_ref=back_send.at[x_to * ny + y_to], dst_ref=back_recv.at[mine],
            send_sem=back_ssem.at[i], recv_sem=back_rsem.at[i],
            device_id=device(x_to, y_to, z, core), device_id_type=MESH,
        )

    backs = [back_copy(i, dx, dy) for i, (dx, dy) in enumerate(xy_offsets)]
    start(backs)
    back_recv[mine] = back_send[mine]
    lax.fori_loop(tiles // 4, tiles, own_tile, 0)

    for copy in pending + shared:
        copy.wait_send()
    for part in range(2):
        for hop in range(1, half + 1):
            for copy in ring_copies(0, hop, part):
                copy.wait_send()
            if hop < half:
                for copy in ring_copies(1, hop, part):
                    copy.wait_send()
    for offset in range(1, nz):
        z_copy(offset).wait_send()

    def gave(index, carry):
        for copy in give_copies(index):
            copy.wait_send()
        return carry

    lax.fori_loop(0, tiles, gave, 0)

    for copy in backs:
        copy.wait_recv()
    for i in range(nx):
        owned = back_recv[i * ny].astype(F32)
        for row_y in range(1, ny):
            owned = owned + back_recv[i * ny + row_y].astype(F32)
        dq_ref[:, 16 * DH * i : 16 * DH * (i + 1)] = (owned * scale).reshape(1, 16 * DH).astype(BF16)
    for copy in backs:
        copy.wait_send()


def fused(nx, ny, nz, slots, tile, lengths, q, m, o, lse, keys, values):
    ctx_len, kv_cols = keys.shape
    unit = slots * 8
    columns = 2 * nz * unit
    vmem = pl.BlockSpec(memory_space=pltpu.VMEM)
    smem = pl.BlockSpec(memory_space=pltpu.SMEM)
    hbm = pl.BlockSpec(memory_space=pl.ANY)
    dma = pltpu.SemaphoreType.DMA
    packets = nx * ny
    half = nz // 2
    tiles = ctx_len // tile
    scratch = [
        pltpu.VMEM((CORES, ctx_len, kv_cols), BF16),
        pltpu.VMEM((CORES, ctx_len, kv_cols), BF16),
    ] + [pltpu.VMEM((ctx_len, kv_cols), BF16)] * 4 + [
        pltpu.VMEM((nx, 32, 128), BF16),
        pltpu.VMEM((nx, 4, 128), F32),
        pltpu.VMEM((packets, 32, 128), BF16),
        pltpu.VMEM((packets, 4, 128), F32),
        pltpu.VMEM((nz, 2, 2, unit, 128), BF16),
        pltpu.VMEM((nz, 4, 128), F32),
        pltpu.VMEM((columns, kv_cols), BF16),
        pltpu.VMEM((columns, kv_cols), BF16),
        pltpu.VMEM((2, columns), F32),
        pltpu.VMEM((CORES, ctx_len, columns), BF16),
        pltpu.VMEM((CORES, ctx_len, columns), BF16),
        pltpu.VMEM((4 * unit, kv_cols), F32),
        pltpu.VMEM((2, unit, 128), F32),
        pltpu.VMEM((nz, 2, unit, 128), BF16),
        pltpu.VMEM((nz, 2, unit, 128), BF16),
        pltpu.VMEM((slots, 16, 128), F32),
        pltpu.VMEM((packets, 16, 128), BF16),
        pltpu.VMEM((packets, 16, 128), BF16),
        dma((2,)), dma((2,)), dma((2,)), dma((2, tiles)), dma((2, tiles)),
        dma((packets,)), dma((packets,)), dma((packets,)), dma((packets,)),
        dma((2, half + 1, 2)), dma((2, half + 1, 2)), dma((2, half + 1)), dma((2, half + 1)),
        dma((nz,)), dma((nz,)),
        dma((packets,)), dma((packets,)),
    ]
    flops = 5 * 2 * ctx_len * 128 * 2 * unit * 2 * nz
    return pl.pallas_call(
        functools.partial(kernel, nx, ny, nz, slots, tile),
        out_shape=(
            pltpu.VMEM(q.shape, BF16),
            pltpu.VMEM(keys.shape, BF16),
            pltpu.VMEM(values.shape, BF16),
        ),
        in_specs=[smem, vmem, vmem, vmem, vmem, hbm, hbm],
        out_specs=(vmem, vmem, vmem),
        scratch_shapes=scratch,
        compiler_params=pltpu.CompilerParams(
            collective_id=0, has_side_effects=True, vmem_limit_bytes=56 << 20
        ),
        cost_estimate=pl.CostEstimate(
            flops=flops, bytes_accessed=8 * ctx_len * kv_cols, transcendentals=0
        ),
    )(lengths, q, m, o, lse, keys, values)


def hand_over_kernel(dq_in, dk_in, dv_in, dq_out, dk_out, dv_out, sems):
    copies = [
        pltpu.make_async_copy(dk_in, dk_out, sems.at[0]),
        pltpu.make_async_copy(dv_in, dv_out, sems.at[1]),
    ]
    for copy in copies:
        copy.start()
    dq_out[...] = dq_in[...]
    for copy in copies:
        copy.wait()


def hand_over(d_q, d_k, d_v):
    vmem = pl.BlockSpec(memory_space=pltpu.VMEM)
    hbm = pl.BlockSpec(memory_space=pl.ANY)
    return pl.pallas_call(
        hand_over_kernel,
        out_shape=tuple(
            pltpu.HBM(a.shape, a.dtype) if i else jax.ShapeDtypeStruct(a.shape, a.dtype)
            for i, a in enumerate((d_q, d_k, d_v))
        ),
        in_specs=[vmem, vmem, vmem],
        out_specs=(vmem, hbm, hbm),
        scratch_shapes=[pltpu.SemaphoreType.DMA((2,))],
        compiler_params=pltpu.CompilerParams(vmem_limit_bytes=8 << 20),
    )(d_q, d_k, d_v)


def solution(mesh, nz=RING, slots=SLOTS, tile=TILE):
    nx = mesh.shape["head"]
    ny = mesh.shape["ctx"] // (nz * CORES)

    def on_device(queries, d_out, out_rows, lse, lengths, keys, values):
        d_q, d_k, d_v = fused(
            nx, ny, nz, slots, tile, lengths,
            queries, d_out, out_rows, lse, keys, values,
        )
        return hand_over(d_q, d_k, d_v)

    rows = P(("head", "ctx"), None)
    return jax.shard_map(
        on_device,
        mesh=mesh,
        in_specs=(rows, rows, rows, rows, P(), P("ctx", "head"), P("ctx", "head")),
        out_specs=(rows, P("ctx", "head"), P("ctx", "head")),
        check_vma=False,
    )
```
